768 devices in a mesh: rep: 16 (over x_lo, y), shard: 48 (over x_hi, z, core).
Axes of the slice: x: 4 (x_hi: 2, x_lo: 2; x = x_hi * 2 + x_lo), y: 8, z: 12, core: 2. Of those that a mesh axis runs over, the one named last changes fastest.
Arguments:
- bag_ids: int32 [49152, 20], P(('rep', 'shard')), may hold values from 0 to 24575
- table: float32 [24576, 256], P('shard'), may hold values from -1.2 to 1.2
- accum: float32 [24576], P('shard'), may hold values from 0.01 to 0.1
- cross_weight: float32 [256, 256], replicated, may hold values from -0.375 to 0.375
- cross_bias: float32 [256], replicated, may hold values from -4 to 4
- upstream: float32 [49152, 256], P(('rep', 'shard')), may hold values from -6 to 6
Outputs:
- crossed: float32 [49152, 256], P(('rep', 'shard'))
- new_table: float32 [24576, 256], P('shard')
- new_accum: float32 [24576], P('shard')
The draws below stay inside these ranges and needn't reach their ends.
All inputs are finite; a program needn't handle non-finite values.
Results may differ from the reference program's by a relative error of at most 0.00014.
Values sent between devices are 32-bit elements; how exact they have to be, the bound alone decides.
No kernel may reach another device: no remote copies, remote signals or barrier semaphores. Data moves between devices by JAX's collectives and lax.ppermute only.
A program may use at most 64 MiB of HBM per device.

```python
import math
import jax
import jax.numpy as jnp
import numpy as np
from jax import lax

E = 256
BAG = 20
ROWS = 24576
SAMPLES = 49152


def set_ends(array, own_key, smallest, high):
    longest = array.shape.index(max(array.shape))
    spots = []
    for shift in (0, 1):
        where = [jax.random.randint(jax.random.fold_in(own_key, axis), (), 0, length) for axis, length in enumerate(array.shape)]
        where[longest] = (where[longest] + shift) % array.shape[longest]
        spots.append(tuple(where))
    return array.at[spots[0]].set(smallest).at[spots[1]].set(high)


def block_scale(rng, extent, cuts, least, top_value):
    gain = 1.0
    for position, shards_of in cuts:
        steps = jax.random.uniform(jax.random.fold_in(jax.random.fold_in(rng, 6), position), (shards_of,), jnp.float32, least / len(cuts), top_value / len(cuts))
        gain = gain * jnp.repeat(jnp.exp(steps), extent[position] // shards_of).reshape((-1,) + (1,) * (len(extent) - 1 - position))
    return gain


def rank_bounds(count, lean):
    weights = [(1 << 20) // math.isqrt(standing ** lean) + 1 for standing in range(1, count + 1)]
    spread = 1 + sum(weights) // (1 << 30)
    return np.cumsum(np.array([max(1, weight // spread) for weight in weights]))


def ranked_ids(stream_key, shape, number_of, slope):
    grid = rank_bounds(number_of, slope)
    lot = jax.random.randint(jax.random.fold_in(stream_key, 1), shape, 0, int(grid[number_of - 1]))
    rank = jnp.searchsorted(jnp.asarray(grid, jnp.int32), lot, side="right")
    return jax.random.permutation(jax.random.fold_in(stream_key, 2), number_of)[rank].astype(jnp.int32)


def scatter_about(rng, shape, spread, reach, shards=(), kind=jnp.bfloat16):
    level = block_scale(rng, shape, shards, -0.22, 0.18) if shards else 1.0
    result = jax.random.normal(rng, shape, jnp.float32) * spread * level
    return jnp.minimum(jnp.maximum(result, -reach), reach).astype(kind)


def setup_inputs(seed: int = 0) -> dict:
    key_of = jax.random.split(jax.random.key(seed), 7)
    return {
        "bag_ids": set_ends(ranked_ids(key_of[0], (SAMPLES, BAG), ROWS, 2), jax.random.fold_in(key_of[0], 3), 0, ROWS - 1).astype(jnp.int32),
        "table": scatter_about(key_of[1], (ROWS, E), 0.2, 1.2, ((0, 48),), jnp.float32),
        "accum": jnp.clip(jnp.exp(math.log(0.1) - 2.3025851 * jax.random.uniform(key_of[2], (ROWS,), jnp.float32) ** block_scale(key_of[2], (ROWS,), ((0, 48),), -0.2, 0.2)), 0.01, 0.1),
        "cross_weight": scatter_about(key_of[3], (E, E), E ** -0.5, 0.375, (), jnp.float32),
        "cross_bias": scatter_about(key_of[4], (E,), 1.0, 4.0, (), jnp.float32),
        "upstream": scatter_about(key_of[5], (SAMPLES, E), 1.0, 6.0, ((0, 768),), jnp.float32),
    }


def reference(bag_ids, table, accum, cross_weight, cross_bias, upstream):
    pooled = lax.optimization_barrier(jnp.sum(jnp.take(table, bag_ids, axis=0), axis=1))
    mixed = jnp.dot(pooled, cross_weight, precision=lax.Precision.HIGHEST) + cross_bias
    crossed = pooled * mixed + pooled
    back = upstream * mixed + jnp.dot(upstream * pooled, cross_weight.T, precision=lax.Precision.HIGHEST) + upstream
    grads = jnp.zeros(table.shape, table.dtype)
    for column in range(BAG):
        grads = grads + jax.ops.segment_sum(back, bag_ids[:, column], num_segments=ROWS)
    new_accum = accum + lax.optimization_barrier(jnp.mean(grads * grads, axis=1))
    new_table = table - 0.5 * grads / jnp.sqrt(new_accum)[:, None]
    return (crossed, new_table, new_accum)
```

```python
import jax
import jax.numpy as jnp
from jax import lax
from jax.experimental import pallas as pl
from jax.experimental.pallas import tpu as pltpu
from jax.sharding import Mesh
from jax.sharding import PartitionSpec as P

AXES = ("xl", "y", "xh", "z", "c")
SIZES = (2, 8, 2, 12, 2)
NZ = 12
LANES = 128
VMEM_LIMIT = 48 * 1024 * 1024


def split_halves(x):
    high = x.astype(jnp.bfloat16)
    return high, (x - high.astype(jnp.float32)).astype(jnp.bfloat16)


def count_kernel(base_ref, ids_ref, out_ref):
    bag = ids_ref.shape[1]
    rows = out_ref.shape[0] // 4
    ids = jnp.concatenate([ids_ref[0], ids_ref[1]], axis=1)
    word = ids & (LANES - 1)
    values = []
    for q in range(4):
        local = ids - base_ref[q]
        inside = (local >= 0) & (local < rows)
        values.append(jnp.where(inside, jnp.int32(1) << ((local & (rows - 1)) >> 7) * 8, 0))
    part = 32
    for first in range(0, LANES, part):
        lines = lax.broadcasted_iota(jnp.int32, (part, LANES), 0) + first
        sums = [jnp.zeros((part, LANES), jnp.int32) for _ in range(4)]
        for j in range(bag):
            hit = word[j : j + 1] == lines
            for q in range(4):
                sums[q] = sums[q] + jnp.where(hit, values[q][j : j + 1], 0)
        for q in range(4):
            for f in range(rows // LANES):
                count = (sums[q] >> (8 * f)) & 255
                at = q * rows + f * LANES + first
                out_ref[at : at + part, :] = count.astype(jnp.float32).astype(jnp.bfloat16)


def count_rows(base, ids, rows):
    blocks, bag, per = ids.shape
    return pl.pallas_call(
        count_kernel,
        out_shape=jax.ShapeDtypeStruct((4 * rows, blocks * per), jnp.bfloat16),
        grid_spec=pltpu.PrefetchScalarGridSpec(
            num_scalar_prefetch=1,
            grid=(blocks // 2,),
            in_specs=[pl.BlockSpec((2, bag, per), lambda i, b: (i, 0, 0))],
            out_specs=pl.BlockSpec((4 * rows, 2 * per), lambda i, b: (0, i)),
        ),
        compiler_params=pltpu.CompilerParams(vmem_limit_bytes=VMEM_LIMIT),
        name="count_rows",
    )(base, ids)


def pool_kernel(xh_ref, counts_ref, own_ref, own_c_ref, far_ref, far_c_ref, out_ref, halves):
    rows, width = own_ref.shape

    @pl.when(pl.program_id(0) == 0)
    def _():
        xh = xh_ref[0]
        for at, ref in (
            (2 * xh, own_ref),
            (2 * xh + 1, own_c_ref),
            (2 - 2 * xh, far_ref),
            (3 - 2 * xh, far_c_ref),
        ):
            high, low = split_halves(ref[...])
            halves[at, :, :width] = high
            halves[at, :, width:] = low

    total = None
    for p in range(4):
        term = lax.dot_general(
            counts_ref[p * rows : (p + 1) * rows, :],
            halves[p],
            (((0,), (0,)), ((), ())),
            preferred_element_type=jnp.float32,
        )
        total = term if total is None else total + term
    out_ref[...] = total[:, :width] + total[:, width:]


def pool(xh, counts, tables, tile=256):
    rows, width = tables[0].shape
    samples = counts.shape[1]
    whole = pl.BlockSpec((rows, width), lambda i, b: (0, 0))
    return pl.pallas_call(
        pool_kernel,
        out_shape=jax.ShapeDtypeStruct((samples, width), jnp.float32),
        grid_spec=pltpu.PrefetchScalarGridSpec(
            num_scalar_prefetch=1,
            grid=(samples // tile,),
            in_specs=[pl.BlockSpec((4 * rows, tile), lambda i, b: (0, i))] + [whole] * 4,
            out_specs=pl.BlockSpec((tile, width), lambda i, b: (i, 0)),
            scratch_shapes=[pltpu.VMEM((4, rows, 2 * width), jnp.bfloat16)],
        ),
        compiler_params=pltpu.CompilerParams(vmem_limit_bytes=VMEM_LIMIT),
        name="pool",
    )(xh, counts, *tables)


def dot3(a, b, dims):
    a_high, a_low = split_halves(a)
    b_high, b_low = split_halves(b)

    def dot(u, v):
        return lax.dot_general(u, v, (dims, ((), ())), preferred_element_type=jnp.float32)

    return dot(a_high, b_high) + (dot(a_high, b_low) + dot(a_low, b_high))


def cross_kernel(parts_ref, weight_ref, bias_ref, upstream_ref, crossed_ref, back_ref):
    pooled = parts_ref[0]
    for k in range(1, parts_ref.shape[0]):
        pooled = pooled + parts_ref[k]
    weight, upstream = weight_ref[...], upstream_ref[...]
    mixed = dot3(pooled, weight, ((1,), (0,))) + bias_ref[...]
    crossed_ref[...] = pooled * mixed + pooled
    back_ref[...] = upstream * mixed + dot3(upstream * pooled, weight, ((1,), (1,))) + upstream


def cross(parts, weight, bias, upstream):
    out = jax.ShapeDtypeStruct(upstream.shape, jnp.float32)
    return pl.pallas_call(
        cross_kernel,
        out_shape=(out, out),
        compiler_params=pltpu.CompilerParams(vmem_limit_bytes=VMEM_LIMIT),
        name="cross",
    )(parts, weight, bias.reshape(1, -1), upstream)


def row_kernel(counts_ref, back_ref, out_ref, halves):
    width = back_ref.shape[1]

    @pl.when(pl.program_id(0) == 0)
    def _():
        high, low = split_halves(back_ref[...])
        halves[:, :width] = high
        halves[:, width:] = low

    both = jnp.dot(counts_ref[...], halves[...], preferred_element_type=jnp.float32)
    out_ref[0] = both[:, :width] + both[:, width:]


def row_sums(counts, back, rows, core):
    samples, width = back.shape
    return pl.pallas_call(
        row_kernel,
        out_shape=jax.ShapeDtypeStruct((2, rows, width), jnp.float32),
        grid=(2,),
        in_specs=[
            pl.BlockSpec((rows, samples), lambda i: (2 * i + core, 0)),
            pl.BlockSpec((samples, width), lambda i: (0, 0)),
        ],
        out_specs=pl.BlockSpec((1, rows, width), lambda i: (i, 0, 0)),
        scratch_shapes=[pltpu.VMEM((samples, 2 * width), jnp.bfloat16)],
        compiler_params=pltpu.CompilerParams(vmem_limit_bytes=VMEM_LIMIT),
        name="row_sums",
    )(counts, back)


def adagrad_rows(rows, sums, grads):
    fresh = sums + jnp.mean(grads * grads, axis=1)
    return (rows - 0.5 * grads / jnp.sqrt(fresh)[:, None], fresh)


def other_core(x):
    return lax.ppermute(x, "c", [(0, 1), (1, 0)])


def body(bag_ids, table, accum, cross_weight, cross_bias, upstream):
    per, bag = bag_ids.shape
    rows, width = table.shape
    xh, z, c = (lax.axis_index(a) for a in ("xh", "z", "c"))
    base = jnp.stack(
        [(h * (NZ * 2) + z * 2 + (c if d == 0 else 1 - c)) * rows for h in (0, 1) for d in (0, 1)]
    ).astype(jnp.int32)

    ids = lax.all_to_all(
        jnp.broadcast_to(bag_ids.T[None], (NZ, bag, per)), "z", 0, 0, tiled=True
    )
    far = lax.ppermute(table, ("xl", "xh"), [(0, 3), (3, 0), (1, 2), (2, 1)])
    tables = (table, other_core(table), far, other_core(far))
    counts = count_rows(base, ids, rows)
    partial = pool(xh.astype(jnp.int32).reshape(1), counts, tables)
    parts = lax.all_to_all(partial.reshape(NZ, per, width), "z", 0, 0, tiled=True)
    crossed, back = cross(parts, cross_weight, cross_bias, upstream)

    gathered = lax.all_gather(back, "z", axis=0, tiled=True)
    theirs = row_sums(counts, gathered, rows, 1)
    mine = row_sums(counts, gathered, rows, 0)
    mine = mine + other_core(theirs)
    blocks = mine.reshape(32, rows // 16, width)
    blocks = lax.all_to_all(blocks, ("xh", "xl", "y"), 0, 0, tiled=True)
    total = jnp.sum(blocks, axis=0)
    totals = lax.all_to_all(
        jnp.broadcast_to(total[None], (16,) + total.shape), ("xl", "y"), 0, 0, tiled=True
    ).reshape(rows, width)
    new_table, new_accum = adagrad_rows(table, accum, totals)
    return (crossed, new_table, new_accum)


def solution(mesh):
    fine = Mesh(mesh.devices.reshape(SIZES), AXES)
    samples = P(AXES, None)
    shard = ("xh", "z", "c")
    return jax.shard_map(
        body,
        mesh=fine,
        in_specs=(samples, P(shard, None), P(shard), P(), P(), samples),
        out_specs=(samples, P(shard, None), P(shard)),
        check_vma=False,
    )
```

```python
import functools

import jax
import jax.numpy as jnp
from jax import lax
from jax.experimental import pallas as pl
from jax.experimental.pallas import tpu as pltpu
from jax.sharding import Mesh
from jax.sharding import PartitionSpec as P

AXES = ("xl", "y", "xh", "z", "c")
SIZES = (2, 8, 2, 12, 2)
NZ = 12
LANES = 128
PARAMS = pltpu.CompilerParams(vmem_limit_bytes=16 * 1024 * 1024)
SCALARS = pl.BlockSpec(memory_space=pltpu.SMEM)
WHOLE = pl.BlockSpec(memory_space=pltpu.VMEM)


def split_halves(x):
    high = x.astype(jnp.bfloat16)
    return high, (x - high.astype(jnp.float32)).astype(jnp.bfloat16)


def count_kernel(bag, per, base_ref, ids_ref, out_ref):
    rows = out_ref.shape[0] // 4
    part = 32

    def two_blocks(i, _):
        ids = jnp.concatenate([ids_ref[2 * i, :, :per], ids_ref[2 * i + 1, :, :per]], axis=1)
        columns = pl.ds(pl.multiple_of(i * LANES, LANES), LANES)
        word = ids & (LANES - 1)
        values = []
        for q in range(4):
            local = ids - base_ref[q]
            inside = (local >= 0) & (local < rows)
            values.append(jnp.where(inside, jnp.int32(1) << ((local & (rows - 1)) >> 7) * 8, 0))
        for first in range(0, LANES, part):
            lines = lax.broadcasted_iota(jnp.int32, (part, LANES), 0) + first
            sums = [jnp.zeros((part, LANES), jnp.int32) for _ in range(4)]
            for j in range(bag):
                hit = word[j : j + 1] == lines
                for q in range(4):
                    sums[q] = sums[q] + jnp.where(hit, values[q][j : j + 1], 0)
            for q in range(4):
                for f in range(rows // LANES):
                    count = (sums[q] >> (8 * f)) & 255
                    at = q * rows + f * LANES + first
                    out_ref[at : at + part, columns] = count.astype(jnp.float32).astype(jnp.bfloat16)
        return 0

    lax.fori_loop(0, ids_ref.shape[0] // 2, two_blocks, 0)


def count_rows(places, ids, bag, per, rows):
    return pl.pallas_call(
        functools.partial(count_kernel, bag, per),
        out_shape=jax.ShapeDtypeStruct((4 * rows, ids.shape[0] * per), jnp.bfloat16),
        in_specs=[SCALARS, WHOLE],
        out_specs=WHOLE,
        compiler_params=PARAMS,
        name="count_rows",
    )(places, ids)


def pool_kernel(tile, places_ref, counts_ref, own_ref, own_c_ref, far_ref, far_c_ref, out_ref, halves):
    rows, width = own_ref.shape
    for place, ref in ((4, own_ref), (5, own_c_ref), (6, far_ref), (7, far_c_ref)):
        high, low = split_halves(ref[...])
        at = places_ref[place]
        halves[at, :, :width] = high
        halves[at, :, width:] = low

    def some_samples(i, _):
        some = pl.ds(pl.multiple_of(i * tile, tile), tile)
        total = None
        for p in range(4):
            term = lax.dot_general(
                counts_ref[p * rows : (p + 1) * rows, some],
                halves[p],
                (((0,), (0,)), ((), ())),
                preferred_element_type=jnp.float32,
            )
            total = term if total is None else total + term
        out_ref[some, :] = total[:, :width] + total[:, width:]
        return 0

    lax.fori_loop(0, counts_ref.shape[1] // tile, some_samples, 0)


def pool(places, counts, tables, tile=256):
    rows, width = tables[0].shape
    return pl.pallas_call(
        functools.partial(pool_kernel, tile),
        out_shape=jax.ShapeDtypeStruct((counts.shape[1], width), jnp.float32),
        in_specs=[SCALARS] + [WHOLE] * 5,
        out_specs=WHOLE,
        scratch_shapes=[pltpu.VMEM((4, rows, 2 * width), jnp.bfloat16)],
        compiler_params=PARAMS,
        name="pool",
    )(places, counts, *tables)


def dot3(a, b, dims):
    a_high, a_low = split_halves(a)
    b_high, b_low = split_halves(b)

    def dot(u, v):
        return lax.dot_general(u, v, (dims, ((), ())), preferred_element_type=jnp.float32)

    return dot(a_high, b_high) + (dot(a_high, b_low) + dot(a_low, b_high))


def cross_kernel(parts_ref, weight_ref, bias_ref, upstream_ref, crossed_ref, back_ref):
    pooled = parts_ref[0]
    for k in range(1, parts_ref.shape[0]):
        pooled = pooled + parts_ref[k]
    weight, upstream = weight_ref[...], upstream_ref[...]
    mixed = dot3(pooled, weight, ((1,), (0,))) + bias_ref[...]
    crossed_ref[...] = pooled * mixed + pooled
    back_ref[...] = upstream * mixed + dot3(upstream * pooled, weight, ((1,), (1,))) + upstream


def cross(parts, weight, bias, upstream):
    out = jax.ShapeDtypeStruct(upstream.shape, jnp.float32)
    return pl.pallas_call(
        cross_kernel,
        out_shape=(out, out),
        compiler_params=PARAMS,
        name="cross",
    )(parts, weight, bias.reshape(1, -1), upstream)


def row_kernel(first, places_ref, counts_ref, back_ref, a_ref, b_ref, halves):
    rows, width = a_ref.shape
    high, low = split_halves(back_ref[...])
    halves[:, :width] = high
    halves[:, width:] = low
    for k, out_ref in enumerate((a_ref, b_ref)):
        lines = pl.ds(pl.multiple_of(places_ref[first + k] * rows, rows), rows)
        both = jnp.dot(counts_ref[lines, :], halves[...], preferred_element_type=jnp.float32)
        out_ref[...] = both[:, :width] + both[:, width:]


def row_sums(first, places, counts, back, rows):
    samples, width = back.shape
    out = jax.ShapeDtypeStruct((rows, width), jnp.float32)
    return pl.pallas_call(
        functools.partial(row_kernel, first),
        out_shape=(out, out),
        in_specs=[SCALARS, WHOLE, WHOLE],
        out_specs=(WHOLE, WHOLE),
        scratch_shapes=[pltpu.VMEM((samples, 2 * width), jnp.bfloat16)],
        compiler_params=PARAMS,
        name="row_sums",
    )(places, counts, back)


def adagrad_rows(rows, sums, grads):
    fresh = sums + jnp.mean(grads * grads, axis=1)
    return (rows - 0.5 * grads / jnp.sqrt(fresh)[:, None], fresh)


def other_core(x):
    return lax.ppermute(x, "c", [(0, 1), (1, 0)])


def x_neighbour(x):
    return lax.ppermute(x, ("xl", "xh"), [(0, 3), (3, 0), (1, 2), (2, 1)])


def body(bag_ids, table, accum, cross_weight, cross_bias, upstream):
    per, bag = bag_ids.shape
    rows, width = table.shape
    xh, z, c = (lax.axis_index(a) for a in ("xh", "z", "c"))
    places = [(h * (NZ * 2) + z * 2 + d) * rows for h in (0, 1) for d in (c, 1 - c)]
    places = jnp.stack(places + [2 * xh, 2 * xh + 1, 2 - 2 * xh, 3 - 2 * xh]).astype(jnp.int32)

    padded = jnp.pad(bag_ids.T, ((0, -bag % 8), (0, LANES - per)))
    ids = lax.all_to_all(jnp.broadcast_to(padded[None], (NZ,) + padded.shape), "z", 0, 0, tiled=True)
    far = x_neighbour(table)
    own_c = other_core(table)
    far, ids, places = lax.optimization_barrier((far, ids, places))
    tables = (table, own_c, far, other_core(far))
    counts = count_rows(places, ids, bag, per, rows)
    partial = pool(places, counts, tables)
    parts = lax.all_to_all(partial.reshape(NZ, per, width), "z", 0, 0, tiled=True)
    crossed, back = cross(parts, cross_weight, cross_bias, upstream)

    gathered = lax.all_gather(back, "z", axis=0, tiled=True)
    mine, theirs = row_sums(6, places, counts, gathered, rows)
    away = x_neighbour(mine + other_core(theirs))
    mine, theirs = row_sums(4, places, counts, gathered, rows)
    here = mine + other_core(theirs) + away
    blocks = lax.all_to_all(here.reshape(16, rows // 16, width), ("xl", "y"), 0, 0, tiled=True)
    total = jnp.sum(blocks, axis=0)
    totals = lax.all_to_all(
        jnp.broadcast_to(total[None], (16,) + total.shape), ("xl", "y"), 0, 0, tiled=True
    ).reshape(rows, width)
    new_table, new_accum = adagrad_rows(table, accum, totals)
    return (crossed, new_table, new_accum)


def solution(mesh):
    fine = Mesh(mesh.devices.reshape(SIZES), AXES)
    samples = P(AXES, None)
    shard = ("xh", "z", "c")
    return jax.shard_map(
        body,
        mesh=fine,
        in_specs=(samples, P(shard, None), P(shard), P(), P(), samples),
        out_specs=(samples, P(shard, None), P(shard)),
        check_vma=False,
    )
```

```python
import functools

import jax
import jax.numpy as jnp
from jax import lax
from jax.experimental import pallas as pl
from jax.experimental.pallas import tpu as pltpu
from jax.sharding import Mesh
from jax.sharding import PartitionSpec as P

AXES = ("xl", "y", "xh", "z", "c")
SIZES = (2, 8, 2, 12, 2)
NZ = 12
LANES = 128
FIELDS, BITS = 6, 5
PARAMS = pltpu.CompilerParams(vmem_limit_bytes=16 * 1024 * 1024)
SCALARS = pl.BlockSpec(memory_space=pltpu.SMEM)
WHOLE = pl.BlockSpec(memory_space=pltpu.VMEM)


def split_halves(x):
    high = x.astype(jnp.bfloat16)
    return high, (x - high.astype(jnp.float32)).astype(jnp.bfloat16)


def spread_kernel(ids_ref, out_ref):
    bag, per = ids_ref.shape
    half = bag // 2
    ids = jnp.concatenate([ids_ref[:half], ids_ref[half:]], axis=1)
    ids = jnp.concatenate([ids, jnp.zeros((out_ref.shape[1] - half, 2 * per), jnp.int32)], axis=0)
    for k in range(out_ref.shape[0]):
        out_ref[k] = ids


def spread(ids, copies):
    bag, per = ids.shape
    return pl.pallas_call(
        spread_kernel,
        out_shape=jax.ShapeDtypeStruct((copies, -(-bag // 16) * 8, 2 * per), jnp.int32),
        in_specs=[WHOLE],
        out_specs=WHOLE,
        compiler_params=PARAMS,
        name="spread",
    )(ids)


def count_kernel(bag, per, base_ref, ids_ref, out_ref):
    assert bag < 1 << BITS
    rows = out_ref.shape[0] // 4
    pieces = 4 * rows // LANES
    words = -(-pieces // FIELDS)
    part = 32

    def two_blocks(i, _):
        one, two = ids_ref[2 * i, : bag // 2], ids_ref[2 * i + 1, : bag // 2]
        ids = jnp.concatenate(
            [
                jnp.concatenate([one[:, :per], two[:, :per]], axis=1),
                jnp.concatenate([one[:, per:], two[:, per:]], axis=1),
            ],
            axis=0,
        )
        columns = pl.ds(pl.multiple_of(i * LANES, LANES), LANES)
        line = ids & (LANES - 1)
        piece = jnp.full(ids.shape, -1, jnp.int32)
        for q in range(4):
            local = ids - base_ref[q]
            piece = jnp.where((local >= 0) & (local < rows), (q * rows + local) >> 7, piece)
        values = []
        for t in range(words):
            field = piece - t * FIELDS
            inside = (field >= 0) & (field < FIELDS) & (piece >= 0)
            values.append(jnp.where(inside, jnp.int32(1) << jnp.where(inside, field, 0) * BITS, 0))
        for first in range(0, LANES, part):
            lines = lax.broadcasted_iota(jnp.int32, (part, LANES), 0) + first
            sums = [jnp.zeros((part, LANES), jnp.int32) for _ in range(words)]
            for j in range(bag):
                hit = line[j : j + 1] == lines
                for t in range(words):
                    sums[t] = sums[t] + jnp.where(hit, values[t][j : j + 1], 0)
            for p in range(pieces):
                count = (sums[p // FIELDS] >> (BITS * (p % FIELDS))) & ((1 << BITS) - 1)
                at = p * LANES + first
                out_ref[at : at + part, columns] = count.astype(jnp.float32).astype(jnp.bfloat16)
        return 0

    lax.fori_loop(0, ids_ref.shape[0] // 2, two_blocks, 0)


def count_rows(places, ids, bag, per, rows):
    return pl.pallas_call(
        functools.partial(count_kernel, bag, per),
        out_shape=jax.ShapeDtypeStruct((4 * rows, ids.shape[0] * per), jnp.bfloat16),
        in_specs=[SCALARS, WHOLE],
        out_specs=WHOLE,
        compiler_params=PARAMS,
        name="count_rows",
    )(places, ids)


def pool_kernel(tile, places_ref, counts_ref, own_ref, own_c_ref, far_ref, far_c_ref, out_ref, halves):
    rows, width = own_ref.shape
    for place, ref in ((4, own_ref), (5, own_c_ref), (6, far_ref), (7, far_c_ref)):
        high, low = split_halves(ref[...])
        at = places_ref[place]
        halves[at, :, :width] = high
        halves[at, :, width:] = low

    def some_samples(i, _):
        some = pl.ds(pl.multiple_of(i * tile, tile), tile)
        total = None
        for p in range(4):
            term = lax.dot_general(
                counts_ref[p * rows : (p + 1) * rows, some],
                halves[p],
                (((0,), (0,)), ((), ())),
                preferred_element_type=jnp.float32,
            )
            total = term if total is None else total + term
        out_ref[some, :] = total[:, :width] + total[:, width:]
        return 0

    lax.fori_loop(0, counts_ref.shape[1] // tile, some_samples, 0)


def pool(places, counts, tables, tile=256):
    rows, width = tables[0].shape
    return pl.pallas_call(
        functools.partial(pool_kernel, tile),
        out_shape=jax.ShapeDtypeStruct((counts.shape[1], width), jnp.float32),
        in_specs=[SCALARS] + [WHOLE] * 5,
        out_specs=WHOLE,
        scratch_shapes=[pltpu.VMEM((4, rows, 2 * width), jnp.bfloat16)],
        compiler_params=PARAMS,
        name="pool",
    )(places, counts, *tables)


def dot3(a, b, dims):
    a_high, a_low = split_halves(a)
    b_high, b_low = split_halves(b)

    def dot(u, v):
        return lax.dot_general(u, v, (dims, ((), ())), preferred_element_type=jnp.float32)

    return dot(a_high, b_high) + (dot(a_high, b_low) + dot(a_low, b_high))


def cross_kernel(places_ref, parts_ref, weight_ref, bias_ref, upstream_ref, crossed_ref, keep_ref, give_ref):
    pooled = parts_ref[0]
    for k in range(1, parts_ref.shape[0]):
        pooled = pooled + parts_ref[k]
    weight, upstream = weight_ref[...], upstream_ref[...]
    mixed = dot3(pooled, weight, ((1,), (0,))) + bias_ref[...]
    crossed_ref[...] = pooled * mixed + pooled
    back = upstream * mixed + dot3(upstream * pooled, weight, ((1,), (1,))) + upstream
    half = keep_ref.shape[1]
    first = places_ref[8] == 0
    keep_ref[...] = jnp.where(first, back[:, :half], back[:, half:])
    give_ref[...] = jnp.where(first, back[:, half:], back[:, :half])


def cross(places, parts, weight, bias, upstream):
    samples, width = upstream.shape
    half = jax.ShapeDtypeStruct((samples, width // 2), jnp.float32)
    return pl.pallas_call(
        cross_kernel,
        out_shape=(jax.ShapeDtypeStruct(upstream.shape, jnp.float32), half, half),
        in_specs=[SCALARS] + [WHOLE] * 4,
        out_specs=(WHOLE, WHOLE, WHOLE),
        compiler_params=PARAMS,
        name="cross",
    )(places, parts, weight, bias.reshape(1, -1), upstream)


def row_kernel(core, near_ref, far_ref, back_ref, out_ref, halves):
    blocks, per, width = back_ref.shape
    per = per // 2
    for b in range(blocks):
        high, low = split_halves(back_ref[b])
        for k in range(2):
            halves[k, b * per : (b + 1) * per, :width] = high[k * per : (k + 1) * per]
            halves[k, b * per : (b + 1) * per, width:] = low[k * per : (k + 1) * per]
    parts, _, lines, _ = out_ref.shape
    rows = parts * lines
    for h in range(2):
        chunk = slice((2 * h + core) * rows, (2 * h + core + 1) * rows)
        both = jnp.dot(near_ref[chunk, :], halves[0], preferred_element_type=jnp.float32)
        both = both + jnp.dot(far_ref[chunk, :], halves[1], preferred_element_type=jnp.float32)
        out_ref[:, h] = (both[:, :width] + both[:, width:]).reshape(parts, lines, width)


def row_sums(core, near, far, back, rows, parts):
    width = back.shape[2]
    return pl.pallas_call(
        functools.partial(row_kernel, core),
        out_shape=jax.ShapeDtypeStruct((parts, 2, rows // parts, width), jnp.float32),
        in_specs=[WHOLE] * 3,
        out_specs=WHOLE,
        scratch_shapes=[pltpu.VMEM((2, near.shape[1], 2 * width), jnp.bfloat16)],
        compiler_params=PARAMS,
        name="row_sums",
    )(near, far, back)


def adagrad_rows(rows, sums, grads):
    fresh = sums + jnp.sum(grads * grads, axis=(0, 2)) / rows.shape[1]
    scale = 0.5 / jnp.sqrt(fresh)[:, None]
    return (rows - jnp.concatenate([grads[0], grads[1]], axis=1) * scale, fresh)


def other_core(x):
    return lax.ppermute(x, "c", [(0, 1), (1, 0)])


def x_neighbour(x):
    return lax.ppermute(x, ("xl", "xh"), [(0, 3), (3, 0), (1, 2), (2, 1)])


def body(bag_ids, table, accum, cross_weight, cross_bias, upstream):
    per, bag = bag_ids.shape
    rows, width = table.shape
    xh, z, c = (lax.axis_index(a) for a in ("xh", "z", "c"))
    places = [(h * (NZ * 2) + z * 2 + d) * rows for h in (0, 1) for d in (c, 1 - c)]
    places = jnp.stack(places + [2 * xh, 2 * xh + 1, 2 - 2 * xh, 3 - 2 * xh, xh]).astype(jnp.int32)

    copies, sent = lax.optimization_barrier((spread(bag_ids.T, NZ), table))
    ids = lax.all_to_all(copies, "z", 0, 0, tiled=True)
    far = x_neighbour(sent)
    own_c = other_core(sent)
    far, ids, places = lax.optimization_barrier((far, ids, places))
    tables = (table, own_c, far, other_core(far))
    far_ids = x_neighbour(ids)
    counts = count_rows(places, ids, bag, per, rows)
    partial = pool(places, counts, tables)
    partial, far_ids = lax.optimization_barrier((partial, far_ids))
    parts = lax.all_to_all(partial.reshape(NZ, per, width), "z", 0, 0, tiled=True)
    crossed, keep, give = cross(places, parts, cross_weight, cross_bias, upstream)
    far_ids, give = lax.optimization_barrier((far_ids, give))
    far_counts = count_rows(places, far_ids, bag, per, rows)

    halves = jnp.concatenate([keep, x_neighbour(give)], axis=0)
    gathered = lax.all_gather(halves, "z", axis=0, tiled=False)
    theirs = other_core(row_sums(1, counts, far_counts, gathered, rows, 16))
    mine = row_sums(0, counts, far_counts, gathered, rows, 16) + theirs
    total = jnp.sum(lax.all_to_all(mine, ("xl", "y"), 0, 0, tiled=False), axis=0)
    copies = jnp.broadcast_to(total[:, None], (2, 16) + total.shape[1:])
    totals = lax.all_to_all(
        copies.reshape((32,) + total.shape[1:]), ("xh", "xl", "y"), 0, 0, tiled=True
    ).reshape(2, rows, width // 2)
    new_table, new_accum = adagrad_rows(table, accum, totals)
    return (crossed, new_table, new_accum)


def solution(mesh):
    fine = Mesh(mesh.devices.reshape(SIZES), AXES)
    samples = P(AXES, None)
    shard = ("xh", "z", "c")
    return jax.shard_map(
        body,
        mesh=fine,
        in_specs=(samples, P(shard, None), P(shard), P(), P(), samples),
        out_specs=(samples, P(shard, None), P(shard)),
        check_vma=False,
    )
```

```python
import functools

import jax
import jax.numpy as jnp
from jax import lax
from jax.experimental import pallas as pl
from jax.experimental.pallas import tpu as pltpu
from jax.sharding import Mesh
from jax.sharding import PartitionSpec as P

AXES = ("xl", "y", "xh", "z", "c")
SIZES = (2, 8, 2, 12, 2)
NZ = 12
LANES = 128
FIELDS, BITS = 6, 5
PARAMS = pltpu.CompilerParams(vmem_limit_bytes=16 * 1024 * 1024)
SCALARS = pl.BlockSpec(memory_space=pltpu.SMEM)
WHOLE = pl.BlockSpec(memory_space=pltpu.VMEM)


def split_halves(x):
    high = x.astype(jnp.bfloat16)
    return high, (x - high.astype(jnp.float32)).astype(jnp.bfloat16)


def spread_kernel(ids_ref, out_ref):
    bag, per = ids_ref.shape
    half = bag // 2
    ids = jnp.concatenate([ids_ref[:half], ids_ref[half:]], axis=1)
    ids = jnp.concatenate([ids, jnp.zeros((out_ref.shape[1] - half, 2 * per), jnp.int32)], axis=0)
    for k in range(out_ref.shape[0]):
        out_ref[k] = ids


def spread(ids, copies):
    bag, per = ids.shape
    return pl.pallas_call(
        spread_kernel,
        out_shape=jax.ShapeDtypeStruct((copies, -(-bag // 16) * 8, 2 * per), jnp.int32),
        in_specs=[WHOLE],
        out_specs=WHOLE,
        compiler_params=PARAMS,
        name="spread",
    )(ids)


def count_kernel(bag, per, base_ref, ids_ref, out_ref):
    assert bag < 1 << BITS
    rows = out_ref.shape[0] // 4
    pieces = 4 * rows // LANES
    words = -(-pieces // FIELDS)
    part = 32

    def two_blocks(i, _):
        one, two = ids_ref[2 * i, : bag // 2], ids_ref[2 * i + 1, : bag // 2]
        ids = jnp.concatenate(
            [
                jnp.concatenate([one[:, :per], two[:, :per]], axis=1),
                jnp.concatenate([one[:, per:], two[:, per:]], axis=1),
            ],
            axis=0,
        )
        columns = pl.ds(pl.multiple_of(i * LANES, LANES), LANES)
        line = ids & (LANES - 1)
        piece = jnp.full(ids.shape, -1, jnp.int32)
        for q in range(4):
            local = ids - base_ref[q]
            piece = jnp.where((local >= 0) & (local < rows), (q * rows + local) >> 7, piece)
        values = []
        for t in range(words):
            field = piece - t * FIELDS
            inside = (field >= 0) & (field < FIELDS) & (piece >= 0)
            values.append(jnp.where(inside, jnp.int32(1) << jnp.where(inside, field, 0) * BITS, 0))
        for first in range(0, LANES, part):
            lines = lax.broadcasted_iota(jnp.int32, (part, LANES), 0) + first
            sums = [jnp.zeros((part, LANES), jnp.int32) for _ in range(words)]
            for j in range(bag):
                hit = line[j : j + 1] == lines
                for t in range(words):
                    sums[t] = sums[t] + jnp.where(hit, values[t][j : j + 1], 0)
            for p in range(pieces):
                count = (sums[p // FIELDS] >> (BITS * (p % FIELDS))) & ((1 << BITS) - 1)
                at = p * LANES + first
                out_ref[at : at + part, columns] = count.astype(jnp.float32).astype(jnp.bfloat16)
        return 0

    lax.fori_loop(0, ids_ref.shape[0] // 2, two_blocks, 0)


def count_rows(places, ids, bag, per, rows):
    return pl.pallas_call(
        functools.partial(count_kernel, bag, per),
        out_shape=jax.ShapeDtypeStruct((4 * rows, ids.shape[0] * per), jnp.bfloat16),
        in_specs=[SCALARS, WHOLE],
        out_specs=WHOLE,
        compiler_params=PARAMS,
        name="count_rows",
    )(places, ids)


def pool_kernel(tile, places_ref, counts_ref, own_ref, own_c_ref, far_ref, far_c_ref, out_ref, halves):
    rows, width = own_ref.shape
    for place, ref in ((4, own_ref), (5, own_c_ref), (6, far_ref), (7, far_c_ref)):
        high, low = split_halves(ref[...])
        at = places_ref[place]
        halves[at, :, :width] = high
        halves[at, :, width:] = low

    def some_samples(i, _):
        some = pl.ds(pl.multiple_of(i * tile, tile), tile)
        total = None
        for p in range(4):
            term = lax.dot_general(
                counts_ref[p * rows : (p + 1) * rows, some],
                halves[p],
                (((0,), (0,)), ((), ())),
                preferred_element_type=jnp.float32,
            )
            total = term if total is None else total + term
        out_ref[some, :] = total[:, :width] + total[:, width:]
        return 0

    lax.fori_loop(0, counts_ref.shape[1] // tile, some_samples, 0)


def pool(places, counts, tables, tile=256):
    rows, width = tables[0].shape
    return pl.pallas_call(
        functools.partial(pool_kernel, tile),
        out_shape=jax.ShapeDtypeStruct((counts.shape[1], width), jnp.float32),
        in_specs=[SCALARS] + [WHOLE] * 5,
        out_specs=WHOLE,
        scratch_shapes=[pltpu.VMEM((4, rows, 2 * width), jnp.bfloat16)],
        compiler_params=PARAMS,
        name="pool",
    )(places, counts, *tables)


def dot3(a, b, dims):
    a_high, a_low = split_halves(a)
    b_high, b_low = split_halves(b)

    def dot(u, v):
        return lax.dot_general(u, v, (dims, ((), ())), preferred_element_type=jnp.float32)

    return dot(a_high, b_high) + (dot(a_high, b_low) + dot(a_low, b_high))


def cross_kernel(places_ref, parts_ref, weight_ref, bias_ref, upstream_ref, crossed_ref, keep_ref, give_ref):
    pooled = parts_ref[0]
    for k in range(1, parts_ref.shape[0]):
        pooled = pooled + parts_ref[k]
    weight, upstream = weight_ref[...], upstream_ref[...]
    mixed = dot3(pooled, weight, ((1,), (0,))) + bias_ref[...]
    crossed_ref[...] = pooled * mixed + pooled
    back = upstream * mixed + dot3(upstream * pooled, weight, ((1,), (1,))) + upstream
    half = keep_ref.shape[1]
    first = places_ref[8] == 0
    keep_ref[...] = jnp.where(first, back[:, :half], back[:, half:])
    give_ref[...] = jnp.where(first, back[:, half:], back[:, :half])


def cross(places, parts, weight, bias, upstream):
    samples, width = upstream.shape
    half = jax.ShapeDtypeStruct((samples, width // 2), jnp.float32)
    return pl.pallas_call(
        cross_kernel,
        out_shape=(jax.ShapeDtypeStruct(upstream.shape, jnp.float32), half, half),
        in_specs=[SCALARS] + [WHOLE] * 4,
        out_specs=(WHOLE, WHOLE, WHOLE),
        compiler_params=PARAMS,
        name="cross",
    )(places, parts, weight, bias.reshape(1, -1), upstream)


def row_kernel(core, near_ref, far_ref, back_ref, out_ref, halves):
    blocks, per, width = back_ref.shape
    per = per // 2
    for b in range(blocks):
        high, low = split_halves(back_ref[b])
        for k in range(2):
            halves[k, b * per : (b + 1) * per, :width] = high[k * per : (k + 1) * per]
            halves[k, b * per : (b + 1) * per, width:] = low[k * per : (k + 1) * per]
    rows = out_ref.shape[1]
    for h in range(2):
        chunk = slice((2 * h + core) * rows, (2 * h + core + 1) * rows)
        both = jnp.dot(near_ref[chunk, :], halves[0], preferred_element_type=jnp.float32)
        both = both + jnp.dot(far_ref[chunk, :], halves[1], preferred_element_type=jnp.float32)
        out_ref[h] = both[:, :width] + both[:, width:]


def row_sums(core, near, far, back, rows):
    width = back.shape[2]
    return pl.pallas_call(
        functools.partial(row_kernel, core),
        out_shape=jax.ShapeDtypeStruct((2, rows, width), jnp.float32),
        in_specs=[WHOLE] * 3,
        out_specs=WHOLE,
        scratch_shapes=[pltpu.VMEM((2, near.shape[1], 2 * width), jnp.bfloat16)],
        compiler_params=PARAMS,
        name="row_sums",
    )(near, far, back)


def merge_kernel(parts_ref, out_ref):
    n, width = parts_ref.shape[0] // 2, parts_ref.shape[2]
    for h in range(2):
        total = parts_ref[h * n]
        for k in range(1, n):
            total = total + parts_ref[h * n + k]
        for k in range(out_ref.shape[0]):
            out_ref[k, :, h * width : (h + 1) * width] = total


def merge(parts, copies):
    _, lines, width = parts.shape
    return pl.pallas_call(
        merge_kernel,
        out_shape=jax.ShapeDtypeStruct((copies, lines, 2 * width), jnp.float32),
        in_specs=[WHOLE],
        out_specs=WHOLE,
        compiler_params=PARAMS,
        name="merge",
    )(parts)


def adagrad_kernel(rows_ref, sums_ref, grads_ref, new_rows_ref, new_sums_ref):
    grads = grads_ref[...]
    lines, width = grads.shape
    at = (lines, lines)
    diagonal = lax.broadcasted_iota(jnp.int32, at, 0) == lax.broadcasted_iota(jnp.int32, at, 1)
    sums = jnp.sum(jnp.where(diagonal, sums_ref[0], 0.0), axis=1, keepdims=True)
    fresh = sums + jnp.sum(grads * grads, axis=1, keepdims=True) / width
    new_rows_ref[...] = rows_ref[...] - 0.5 * grads / jnp.sqrt(fresh)
    new_sums_ref[0] = jnp.sum(jnp.where(diagonal, fresh, 0.0), axis=0, keepdims=True)


def adagrad(rows, sums, grads):
    count, width = rows.shape
    block = pl.BlockSpec((LANES, width), lambda i: (i, 0))
    line = pl.BlockSpec((1, 1, LANES), lambda i: (i, 0, 0))
    new_rows, new_sums = pl.pallas_call(
        adagrad_kernel,
        out_shape=(
            jax.ShapeDtypeStruct(rows.shape, jnp.float32),
            jax.ShapeDtypeStruct((count // LANES, 1, LANES), jnp.float32),
        ),
        grid=(count // LANES,),
        in_specs=[block, line, block],
        out_specs=(block, line),
        compiler_params=PARAMS,
        name="adagrad",
    )(rows, sums.reshape(-1, 1, LANES), grads)
    return new_rows, new_sums.reshape(-1)


def other_core(x):
    return lax.ppermute(x, "c", [(0, 1), (1, 0)])


def x_neighbour(x):
    return lax.ppermute(x, ("xl", "xh"), [(0, 3), (3, 0), (1, 2), (2, 1)])


def body(bag_ids, table, accum, cross_weight, cross_bias, upstream):
    per, bag = bag_ids.shape
    rows, width = table.shape
    xh, z, c = (lax.axis_index(a) for a in ("xh", "z", "c"))
    places = [(h * (NZ * 2) + z * 2 + d) * rows for h in (0, 1) for d in (c, 1 - c)]
    places = jnp.stack(places + [2 * xh, 2 * xh + 1, 2 - 2 * xh, 3 - 2 * xh, xh]).astype(jnp.int32)

    copies, sent = lax.optimization_barrier((spread(bag_ids.T, NZ), table))
    ids = lax.all_to_all(copies, "z", 0, 0, tiled=True)
    far = x_neighbour(sent)
    own_c = other_core(sent)
    far, ids, places = lax.optimization_barrier((far, ids, places))
    tables = (table, own_c, far, other_core(far))
    far_ids = x_neighbour(ids)
    counts = count_rows(places, ids, bag, per, rows)
    partial = pool(places, counts, tables)
    partial, far_ids = lax.optimization_barrier((partial, far_ids))
    parts = lax.all_to_all(partial.reshape(NZ, per, width), "z", 0, 0, tiled=True)
    crossed, keep, give = cross(places, parts, cross_weight, cross_bias, upstream)
    far_ids, give = lax.optimization_barrier((far_ids, give))
    far_counts = count_rows(places, far_ids, bag, per, rows)

    halves = jnp.concatenate([keep, x_neighbour(give)], axis=0)
    gathered = lax.all_gather(halves, "z", axis=0, tiled=False)
    theirs = other_core(row_sums(1, counts, far_counts, gathered, rows))
    mine = row_sums(0, counts, far_counts, gathered, rows) + theirs
    part = rows // 16
    got = lax.all_to_all(mine.reshape(32, part, width // 2), ("xh", "xl", "y"), 0, 0, tiled=True)
    totals = lax.all_to_all(merge(got, 16), ("xl", "y"), 0, 0, tiled=True).reshape(rows, width)
    new_table, new_accum = adagrad(table, accum, totals)
    return (crossed, new_table, new_accum)


def solution(mesh):
    fine = Mesh(mesh.devices.reshape(SIZES), AXES)
    samples = P(AXES, None)
    shard = ("xh", "z", "c")
    return jax.shard_map(
        body,
        mesh=fine,
        in_specs=(samples, P(shard, None), P(shard), P(), P(), samples),
        out_specs=(samples, P(shard, None), P(shard)),
        check_vma=False,
    )
```

```python
import functools

import jax
import jax.numpy as jnp
from jax import lax
from jax.experimental import pallas as pl
from jax.experimental.pallas import tpu as pltpu
from jax.sharding import Mesh
from jax.sharding import PartitionSpec as P

AXES = ("xl", "y", "xh", "z", "c")
SIZES = (2, 8, 2, 12, 2)
NZ = 12
LANES = 128
FIELDS, BITS = 6, 5
PARAMS = pltpu.CompilerParams(vmem_limit_bytes=16 * 1024 * 1024)
SCALARS = pl.BlockSpec(memory_space=pltpu.SMEM)
WHOLE = pl.BlockSpec(memory_space=pltpu.VMEM)


def split_halves(x):
    high = x.astype(jnp.bfloat16)
    return high, (x - high.astype(jnp.float32)).astype(jnp.bfloat16)


def spread_kernel(ids_ref, out_ref):
    bag, per = ids_ref.shape
    half = bag // 2
    ids = jnp.concatenate([ids_ref[:half], ids_ref[half:]], axis=1)
    ids = jnp.concatenate([ids, jnp.zeros((out_ref.shape[1] - half, 2 * per), jnp.int32)], axis=0)
    for k in range(out_ref.shape[0]):
        out_ref[k] = ids


def spread(ids, copies):
    bag, per = ids.shape
    return pl.pallas_call(
        spread_kernel,
        out_shape=jax.ShapeDtypeStruct((copies, -(-bag // 16) * 8, 2 * per), jnp.int32),
        in_specs=[WHOLE],
        out_specs=WHOLE,
        compiler_params=PARAMS,
        name="spread",
    )(ids)


def count_kernel(bag, per, base_ref, ids_ref, out_ref):
    assert bag < 1 << BITS
    rows = out_ref.shape[0] // 4
    pieces = 4 * rows // LANES
    words = -(-pieces // FIELDS)
    part = 32

    def two_blocks(i, _):
        one, two = ids_ref[2 * i, : bag // 2], ids_ref[2 * i + 1, : bag // 2]
        ids = jnp.concatenate(
            [
                jnp.concatenate([one[:, :per], two[:, :per]], axis=1),
                jnp.concatenate([one[:, per:], two[:, per:]], axis=1),
            ],
            axis=0,
        )
        columns = pl.ds(pl.multiple_of(i * LANES, LANES), LANES)
        line = ids & (LANES - 1)
        piece = jnp.full(ids.shape, -1, jnp.int32)
        for q in range(4):
            local = ids - base_ref[q]
            piece = jnp.where((local >= 0) & (local < rows), (q * rows + local) >> 7, piece)
        values = []
        for t in range(words):
            field = piece - t * FIELDS
            inside = (field >= 0) & (field < FIELDS) & (piece >= 0)
            values.append(jnp.where(inside, jnp.int32(1) << jnp.where(inside, field, 0) * BITS, 0))
        for first in range(0, LANES, part):
            lines = lax.broadcasted_iota(jnp.int32, (part, LANES), 0) + first
            sums = [jnp.zeros((part, LANES), jnp.int32) for _ in range(words)]
            for j in range(bag):
                hit = line[j : j + 1] == lines
                for t in range(words):
                    sums[t] = sums[t] + jnp.where(hit, values[t][j : j + 1], 0)
            for p in range(pieces):
                count = (sums[p // FIELDS] >> (BITS * (p % FIELDS))) & ((1 << BITS) - 1)
                at = p * LANES + first
                out_ref[at : at + part, columns] = count.astype(jnp.float32).astype(jnp.bfloat16)
        return 0

    lax.fori_loop(0, ids_ref.shape[0] // 2, two_blocks, 0)


def count_rows(places, ids, bag, per, rows):
    return pl.pallas_call(
        functools.partial(count_kernel, bag, per),
        out_shape=jax.ShapeDtypeStruct((4 * rows, ids.shape[0] * per), jnp.bfloat16),
        in_specs=[SCALARS, WHOLE],
        out_specs=WHOLE,
        compiler_params=PARAMS,
        name="count_rows",
    )(places, ids)


def pool_kernel(tile, places_ref, counts_ref, own_ref, own_c_ref, far_ref, far_c_ref, out_ref, halves):
    rows, width = own_ref.shape
    for place, ref in ((4, own_ref), (5, own_c_ref), (6, far_ref), (7, far_c_ref)):
        high, low = split_halves(ref[...])
        at = places_ref[place]
        halves[at, :, :width] = high
        halves[at, :, width:] = low

    def some_samples(i, _):
        some = pl.ds(pl.multiple_of(i * tile, tile), tile)
        total = None
        for p in range(4):
            term = lax.dot_general(
                counts_ref[p * rows : (p + 1) * rows, some],
                halves[p],
                (((0,), (0,)), ((), ())),
                preferred_element_type=jnp.float32,
            )
            total = term if total is None else total + term
        out_ref[some, :] = total[:, :width] + total[:, width:]
        return 0

    lax.fori_loop(0, counts_ref.shape[1] // tile, some_samples, 0)


def pool(places, counts, tables, tile=256):
    rows, width = tables[0].shape
    return pl.pallas_call(
        functools.partial(pool_kernel, tile),
        out_shape=jax.ShapeDtypeStruct((counts.shape[1], width), jnp.float32),
        in_specs=[SCALARS] + [WHOLE] * 5,
        out_specs=WHOLE,
        scratch_shapes=[pltpu.VMEM((4, rows, 2 * width), jnp.bfloat16)],
        compiler_params=PARAMS,
        name="pool",
    )(places, counts, *tables)


def dot3(a, b, dims):
    a_high, a_low = split_halves(a)
    b_high, b_low = split_halves(b)

    def dot(u, v):
        return lax.dot_general(u, v, (dims, ((), ())), preferred_element_type=jnp.float32)

    return dot(a_high, b_high) + (dot(a_high, b_low) + dot(a_low, b_high))


def cross_kernel(places_ref, parts_ref, weight_ref, bias_ref, upstream_ref, crossed_ref, keep_ref, give_ref):
    pooled = parts_ref[0]
    for k in range(1, parts_ref.shape[0]):
        pooled = pooled + parts_ref[k]
    weight, upstream = weight_ref[...], upstream_ref[...]
    mixed = dot3(pooled, weight, ((1,), (0,))) + bias_ref[...]
    crossed_ref[...] = pooled * mixed + pooled
    back = upstream * mixed + dot3(upstream * pooled, weight, ((1,), (1,))) + upstream
    half = keep_ref.shape[1]
    first = places_ref[8] == 0
    keep_ref[...] = jnp.where(first, back[:, :half], back[:, half:])
    give_ref[...] = jnp.where(first, back[:, half:], back[:, :half])


def cross(places, parts, weight, bias, upstream):
    samples, width = upstream.shape
    half = jax.ShapeDtypeStruct((samples, width // 2), jnp.float32)
    return pl.pallas_call(
        cross_kernel,
        out_shape=(jax.ShapeDtypeStruct(upstream.shape, jnp.float32), half, half),
        in_specs=[SCALARS] + [WHOLE] * 4,
        out_specs=(WHOLE, WHOLE, WHOLE),
        compiler_params=PARAMS,
        name="cross",
    )(places, parts, weight, bias.reshape(1, -1), upstream)


def row_kernel(core, near_ref, far_ref, back_ref, out_ref, halves):
    blocks, per, width = back_ref.shape
    per = per // 2
    for b in range(blocks):
        high, low = split_halves(back_ref[b])
        for k in range(2):
            halves[k, b * per : (b + 1) * per, :width] = high[k * per : (k + 1) * per]
            halves[k, b * per : (b + 1) * per, width:] = low[k * per : (k + 1) * per]
    rows = out_ref.shape[1]
    for h in range(2):
        chunk = slice((2 * h + core) * rows, (2 * h + core + 1) * rows)
        both = jnp.dot(near_ref[chunk, :], halves[0], preferred_element_type=jnp.float32)
        both = both + jnp.dot(far_ref[chunk, :], halves[1], preferred_element_type=jnp.float32)
        out_ref[h] = both[:, :width] + both[:, width:]


def row_sums(core, near, far, back, rows):
    width = back.shape[2]
    return pl.pallas_call(
        functools.partial(row_kernel, core),
        out_shape=jax.ShapeDtypeStruct((2, rows, width), jnp.float32),
        in_specs=[WHOLE] * 3,
        out_specs=WHOLE,
        scratch_shapes=[pltpu.VMEM((2, near.shape[1], 2 * width), jnp.bfloat16)],
        compiler_params=PARAMS,
        name="row_sums",
    )(near, far, back)


def merge_kernel(parts_ref, out_ref):
    total = parts_ref[0]
    for k in range(1, parts_ref.shape[0]):
        total = total + parts_ref[k]
    for k in range(out_ref.shape[0]):
        out_ref[k] = total


def merge(parts, copies):
    return pl.pallas_call(
        merge_kernel,
        out_shape=jax.ShapeDtypeStruct((copies,) + parts.shape[1:], jnp.float32),
        in_specs=[WHOLE],
        out_specs=WHOLE,
        compiler_params=PARAMS,
        name="merge",
    )(parts)


def adagrad_kernel(rows_ref, sums_ref, grads_ref, new_rows_ref, new_sums_ref):
    lines, width = rows_ref.shape
    half = width // 2
    at = (lines, lines)
    diagonal = lax.broadcasted_iota(jnp.int32, at, 0) == lax.broadcasted_iota(jnp.int32, at, 1)
    sums = jnp.sum(jnp.where(diagonal, sums_ref[0], 0.0), axis=1, keepdims=True)
    one, two = grads_ref[0], grads_ref[1]
    fresh = sums + jnp.sum(one * one + two * two, axis=1, keepdims=True) / width
    root = jnp.sqrt(fresh)
    new_rows_ref[:, :half] = rows_ref[:, :half] - 0.5 * one / root
    new_rows_ref[:, half:] = rows_ref[:, half:] - 0.5 * two / root
    new_sums_ref[0] = jnp.sum(jnp.where(diagonal, fresh, 0.0), axis=0, keepdims=True)


def adagrad(rows, sums, grads):
    count, width = rows.shape
    block = pl.BlockSpec((LANES, width), lambda i: (i, 0))
    line = pl.BlockSpec((1, 1, LANES), lambda i: (i, 0, 0))
    new_rows, new_sums = pl.pallas_call(
        adagrad_kernel,
        out_shape=(
            jax.ShapeDtypeStruct(rows.shape, jnp.float32),
            jax.ShapeDtypeStruct((count // LANES, 1, LANES), jnp.float32),
        ),
        grid=(count // LANES,),
        in_specs=[block, line, pl.BlockSpec((2, LANES, width // 2), lambda i: (0, i, 0))],
        out_specs=(block, line),
        compiler_params=PARAMS,
        name="adagrad",
    )(rows, sums.reshape(-1, 1, LANES), grads)
    return new_rows, new_sums.reshape(-1)


def other_core(x):
    return lax.ppermute(x, "c", [(0, 1), (1, 0)])


def xl_mate(x):
    return lax.ppermute(x, "xl", [(0, 1), (1, 0)])


def x_neighbour(x):
    return lax.ppermute(x, ("xl", "xh"), [(0, 3), (3, 0), (1, 2), (2, 1)])


def body(bag_ids, table, accum, cross_weight, cross_bias, upstream):
    per, bag = bag_ids.shape
    rows, width = table.shape
    xl, xh, z, c = (lax.axis_index(a) for a in ("xl", "xh", "z", "c"))
    places = [(h * (NZ * 2) + z * 2 + d) * rows for h in (0, 1) for d in (c, 1 - c)]
    places = jnp.stack(places + [2 * xh, 2 * xh + 1, 2 - 2 * xh, 3 - 2 * xh, xl]).astype(jnp.int32)

    copies, sent = lax.optimization_barrier((spread(bag_ids.T, NZ), table))
    ids = lax.all_to_all(copies, "z", 0, 0, tiled=True)
    far = x_neighbour(sent)
    own_c = other_core(sent)
    far, ids, places = lax.optimization_barrier((far, ids, places))
    tables = (table, own_c, far, other_core(far))
    mate_ids = xl_mate(ids)
    counts = count_rows(places, ids, bag, per, rows)
    partial = pool(places, counts, tables)
    partial, mate_ids = lax.optimization_barrier((partial, mate_ids))
    parts = lax.all_to_all(partial.reshape(NZ, per, width), "z", 0, 0, tiled=True)
    crossed, keep, give = cross(places, parts, cross_weight, cross_bias, upstream)
    mate_ids, give = lax.optimization_barrier((mate_ids, give))
    mate_counts = count_rows(places, mate_ids, bag, per, rows)

    halves = jnp.concatenate([keep, xl_mate(give)], axis=0)
    gathered = lax.all_gather(halves, "z", axis=0, tiled=False)
    theirs = other_core(row_sums(1, counts, mate_counts, gathered, rows))
    mine = row_sums(0, counts, mate_counts, gathered, rows) + theirs
    parts = lax.all_to_all(mine.reshape(16, rows // 8, width // 2), ("xh", "y"), 0, 0, tiled=True)
    totals = lax.all_to_all(merge(parts, 16), ("xl", "y"), 0, 0, tiled=True)
    new_table, new_accum = adagrad(table, accum, totals.reshape(2, rows, width // 2))
    return (crossed, new_table, new_accum)


def solution(mesh):
    fine = Mesh(mesh.devices.reshape(SIZES), AXES)
    samples = P(AXES, None)
    shard = ("xh", "z", "c")
    return jax.shard_map(
        body,
        mesh=fine,
        in_specs=(samples, P(shard, None), P(shard), P(), P(), samples),
        out_specs=(samples, P(shard, None), P(shard)),
        check_vma=False,
    )
```

```python
import functools

import jax
import jax.numpy as jnp
from jax import lax
from jax.experimental import pallas as pl
from jax.experimental.pallas import tpu as pltpu
from jax.sharding import Mesh
from jax.sharding import PartitionSpec as P

AXES = ("xl", "y", "xh", "z", "c")
SIZES = (2, 8, 2, 12, 2)
NZ = 12
LANES = 128
FIELDS, BITS = 6, 5
PARAMS = pltpu.CompilerParams(vmem_limit_bytes=16 * 1024 * 1024)
SCALARS = pl.BlockSpec(memory_space=pltpu.SMEM)
WHOLE = pl.BlockSpec(memory_space=pltpu.VMEM)


def split_halves(x):
    high = x.astype(jnp.bfloat16)
    return high, (x - high.astype(jnp.float32)).astype(jnp.bfloat16)


def spread_kernel(ids_ref, out_ref):
    bag, per = ids_ref.shape
    half = bag // 2
    ids = jnp.concatenate([ids_ref[:half], ids_ref[half:]], axis=1)
    for j in range(half):
        out_ref[:, :, j * 2 * per : (j + 1) * 2 * per] = jnp.broadcast_to(
            ids[j : j + 1][None], (out_ref.shape[0], 1, 2 * per)
        )


def spread(ids, copies):
    bag, per = ids.shape
    return pl.pallas_call(
        spread_kernel,
        out_shape=jax.ShapeDtypeStruct((copies, 1, bag * per), jnp.int32),
        in_specs=[WHOLE],
        out_specs=WHOLE,
        compiler_params=PARAMS,
        name="spread",
    )(ids)


def count_kernel(bag, per, base_ref, ids_ref, out_ref):
    assert bag < 1 << BITS
    rows = out_ref.shape[0] // 4
    pieces = 4 * rows // LANES
    words = -(-pieces // FIELDS)
    part = 32

    def two_blocks(i, _):
        one, two = (
            jnp.concatenate([ids_ref[2 * i + k, :, j * 2 * per : (j + 1) * 2 * per] for j in range(bag // 2)], axis=0)
            for k in range(2)
        )
        ids = jnp.concatenate(
            [
                jnp.concatenate([one[:, :per], two[:, :per]], axis=1),
                jnp.concatenate([one[:, per:], two[:, per:]], axis=1),
            ],
            axis=0,
        )
        columns = pl.ds(pl.multiple_of(i * LANES, LANES), LANES)
        line = ids & (LANES - 1)
        piece = jnp.full(ids.shape, -1, jnp.int32)
        for q in range(4):
            local = ids - base_ref[q]
            piece = jnp.where((local >= 0) & (local < rows), (q * rows + local) >> 7, piece)
        values = []
        for t in range(words):
            field = piece - t * FIELDS
            inside = (field >= 0) & (field < FIELDS) & (piece >= 0)
            values.append(jnp.where(inside, jnp.int32(1) << jnp.where(inside, field, 0) * BITS, 0))
        for first in range(0, LANES, part):
            lines = lax.broadcasted_iota(jnp.int32, (part, LANES), 0) + first
            sums = [jnp.zeros((part, LANES), jnp.int32) for _ in range(words)]
            for j in range(bag):
                hit = line[j : j + 1] == lines
                for t in range(words):
                    sums[t] = sums[t] + jnp.where(hit, values[t][j : j + 1], 0)
            for p in range(pieces):
                count = (sums[p // FIELDS] >> (BITS * (p % FIELDS))) & ((1 << BITS) - 1)
                at = p * LANES + first
                out_ref[at : at + part, columns] = count.astype(jnp.float32).astype(jnp.bfloat16)
        return 0

    lax.fori_loop(0, ids_ref.shape[0] // 2, two_blocks, 0)


def count_rows(places, ids, bag, per, rows):
    return pl.pallas_call(
        functools.partial(count_kernel, bag, per),
        out_shape=jax.ShapeDtypeStruct((4 * rows, ids.shape[0] * per), jnp.bfloat16),
        in_specs=[SCALARS, WHOLE],
        out_specs=WHOLE,
        compiler_params=PARAMS,
        name="count_rows",
    )(places, ids)


def pool_kernel(places_ref, counts_ref, own_ref, own_c_ref, far_ref, far_c_ref, out_ref, halves):
    rows, width = own_ref.shape
    for place, ref in ((4, own_ref), (5, own_c_ref), (6, far_ref), (7, far_c_ref)):
        high, low = split_halves(ref[...])
        lines = pl.ds(pl.multiple_of(places_ref[place] * rows, rows), rows)
        halves[lines, :width] = high
        halves[lines, width:] = low
    both = lax.dot_general(
        counts_ref[...], halves[...], (((0,), (0,)), ((), ())), preferred_element_type=jnp.float32
    )
    out_ref[...] = both[:, :width] + both[:, width:]


def pool(places, counts, tables):
    rows, width = tables[0].shape
    return pl.pallas_call(
        pool_kernel,
        out_shape=jax.ShapeDtypeStruct((counts.shape[1], width), jnp.float32),
        in_specs=[SCALARS] + [WHOLE] * 5,
        out_specs=WHOLE,
        scratch_shapes=[pltpu.VMEM((4 * rows, 2 * width), jnp.bfloat16)],
        compiler_params=PARAMS,
        name="pool",
    )(places, counts, *tables)


def dot3(a, b, dims):
    a_high, a_low = split_halves(a)
    b_high, b_low = split_halves(b)

    def dot(u, v):
        return lax.dot_general(u, v, (dims, ((), ())), preferred_element_type=jnp.float32)

    return dot(a_high, b_high) + (dot(a_high, b_low) + dot(a_low, b_high))


def cross_kernel(places_ref, parts_ref, weight_ref, bias_ref, upstream_ref, crossed_ref, keep_ref, give_ref):
    pooled = parts_ref[0]
    for k in range(1, parts_ref.shape[0]):
        pooled = pooled + parts_ref[k]
    weight, upstream = weight_ref[...], upstream_ref[...]
    mixed = dot3(pooled, weight, ((1,), (0,))) + bias_ref[...]
    crossed_ref[...] = pooled * mixed + pooled
    back = upstream * mixed + dot3(upstream * pooled, weight, ((1,), (1,))) + upstream
    half = keep_ref.shape[1]
    first = places_ref[8] == 0
    keep_ref[...] = jnp.where(first, back[:, :half], back[:, half:])
    give_ref[...] = jnp.where(first, back[:, half:], back[:, :half])


def cross(places, parts, weight, bias, upstream):
    samples, width = upstream.shape
    half = jax.ShapeDtypeStruct((samples, width // 2), jnp.float32)
    return pl.pallas_call(
        cross_kernel,
        out_shape=(jax.ShapeDtypeStruct(upstream.shape, jnp.float32), half, half),
        in_specs=[SCALARS] + [WHOLE] * 4,
        out_specs=(WHOLE, WHOLE, WHOLE),
        compiler_params=PARAMS,
        name="cross",
    )(places, parts, weight, bias.reshape(1, -1), upstream)


def row_kernel(core, near_ref, far_ref, back_ref, out_ref, halves):
    blocks, per, width = back_ref.shape
    per = per // 2
    for b in range(blocks):
        high, low = split_halves(back_ref[b])
        for k in range(2):
            halves[k, b * per : (b + 1) * per, :width] = high[k * per : (k + 1) * per]
            halves[k, b * per : (b + 1) * per, width:] = low[k * per : (k + 1) * per]
    rows = out_ref.shape[1]
    for h in range(2):
        chunk = slice((2 * h + core) * rows, (2 * h + core + 1) * rows)
        both = jnp.dot(near_ref[chunk, :], halves[0], preferred_element_type=jnp.float32)
        both = both + jnp.dot(far_ref[chunk, :], halves[1], preferred_element_type=jnp.float32)
        out_ref[h] = both[:, :width] + both[:, width:]


def row_sums(core, near, far, back, rows):
    width = back.shape[2]
    return pl.pallas_call(
        functools.partial(row_kernel, core),
        out_shape=jax.ShapeDtypeStruct((2, rows, width), jnp.float32),
        in_specs=[WHOLE] * 3,
        out_specs=WHOLE,
        scratch_shapes=[pltpu.VMEM((2, near.shape[1], 2 * width), jnp.bfloat16)],
        compiler_params=PARAMS,
        name="row_sums",
    )(near, far, back)


def merge_kernel(parts_ref, out_ref):
    total = parts_ref[0]
    for k in range(1, parts_ref.shape[0]):
        total = total + parts_ref[k]
    for k in range(out_ref.shape[0]):
        out_ref[k] = total


def merge(parts, copies):
    return pl.pallas_call(
        merge_kernel,
        out_shape=jax.ShapeDtypeStruct((copies,) + parts.shape[1:], jnp.float32),
        in_specs=[WHOLE],
        out_specs=WHOLE,
        compiler_params=PARAMS,
        name="merge",
    )(parts)


def adagrad_kernel(rows_ref, sums_ref, grads_ref, new_rows_ref, new_sums_ref):
    lines, width = rows_ref.shape
    half = width // 2
    at = (lines, lines)
    diagonal = lax.broadcasted_iota(jnp.int32, at, 0) == lax.broadcasted_iota(jnp.int32, at, 1)
    sums = jnp.sum(jnp.where(diagonal, sums_ref[0], 0.0), axis=1, keepdims=True)
    one, two = grads_ref[0], grads_ref[1]
    fresh = sums + jnp.sum(one * one + two * two, axis=1, keepdims=True) / width
    root = jnp.sqrt(fresh)
    new_rows_ref[:, :half] = rows_ref[:, :half] - 0.5 * one / root
    new_rows_ref[:, half:] = rows_ref[:, half:] - 0.5 * two / root
    new_sums_ref[0] = jnp.sum(jnp.where(diagonal, fresh, 0.0), axis=0, keepdims=True)


def adagrad(rows, sums, grads):
    count, width = rows.shape
    lines = 2 * LANES
    block = pl.BlockSpec((lines, width), lambda i: (i, 0))
    line = pl.BlockSpec((1, 1, lines), lambda i: (i, 0, 0))
    new_rows, new_sums = pl.pallas_call(
        adagrad_kernel,
        out_shape=(
            jax.ShapeDtypeStruct(rows.shape, jnp.float32),
            jax.ShapeDtypeStruct((count // lines, 1, lines), jnp.float32),
        ),
        grid=(count // lines,),
        in_specs=[block, line, pl.BlockSpec((2, lines, width // 2), lambda i: (0, i, 0))],
        out_specs=(block, line),
        compiler_params=PARAMS,
        name="adagrad",
    )(rows, sums.reshape(-1, 1, lines), grads)
    return new_rows, new_sums.reshape(-1)


def other_core(x):
    return lax.ppermute(x, "c", [(0, 1), (1, 0)])


def xl_mate(x):
    return lax.ppermute(x, "xl", [(0, 1), (1, 0)])


def x_neighbour(x):
    return lax.ppermute(x, ("xl", "xh"), [(0, 3), (3, 0), (1, 2), (2, 1)])


def body(bag_ids, table, accum, cross_weight, cross_bias, upstream):
    per, bag = bag_ids.shape
    rows, width = table.shape
    xl, xh, z, c = (lax.axis_index(a) for a in ("xl", "xh", "z", "c"))
    places = [(h * (NZ * 2) + z * 2 + d) * rows for h in (0, 1) for d in (c, 1 - c)]
    places = jnp.stack(places + [2 * xh, 2 * xh + 1, 2 - 2 * xh, 3 - 2 * xh, xl]).astype(jnp.int32)

    ids = lax.all_to_all(spread(bag_ids.T, NZ), "z", 0, 0, tiled=True)
    far = x_neighbour(table)
    own_c = other_core(table)
    far, ids, places = lax.optimization_barrier((far, ids, places))
    tables = (table, own_c, far, other_core(far))
    mate_ids = xl_mate(ids)
    counts = count_rows(places, ids, bag, per, rows)
    partial = pool(places, counts, tables)
    partial, mate_ids = lax.optimization_barrier((partial, mate_ids))
    parts = lax.all_to_all(partial.reshape(NZ, per, width), "z", 0, 0, tiled=True)
    crossed, keep, give = cross(places, parts, cross_weight, cross_bias, upstream)
    mate_ids, give = lax.optimization_barrier((mate_ids, give))
    mate_counts = count_rows(places, mate_ids, bag, per, rows)

    halves = jnp.concatenate([keep, xl_mate(give)], axis=0)
    gathered = lax.all_gather(halves, "z", axis=0, tiled=False)
    theirs = other_core(row_sums(1, counts, mate_counts, gathered, rows))
    mine = row_sums(0, counts, mate_counts, gathered, rows) + theirs
    parts = lax.all_to_all(mine.reshape(16, rows // 8, width // 2), ("xh", "y"), 0, 0, tiled=True)
    totals = lax.all_to_all(merge(parts, 16), ("xl", "y"), 0, 0, tiled=True)
    new_table, new_accum = adagrad(table, accum, totals.reshape(2, rows, width // 2))
    return (crossed, new_table, new_accum)


def solution(mesh):
    fine = Mesh(mesh.devices.reshape(SIZES), AXES)
    samples = P(AXES, None)
    shard = ("xh", "z", "c")
    return jax.shard_map(
        body,
        mesh=fine,
        in_specs=(samples, P(shard, None), P(shard), P(), P(), samples),
        out_specs=(samples, P(shard, None), P(shard)),
        check_vma=False,
    )
```

```python
import functools

import jax
import jax.numpy as jnp
from jax import lax
from jax.experimental import pallas as pl
from jax.experimental.pallas import tpu as pltpu
from jax.sharding import Mesh
from jax.sharding import PartitionSpec as P

AXES = ("xl", "y", "xh", "z", "c")
SIZES = (2, 8, 2, 12, 2)
NZ = 12
LANES = 128
PARAMS = pltpu.CompilerParams(vmem_limit_bytes=16 * 1024 * 1024)
SCALARS = pl.BlockSpec(memory_space=pltpu.SMEM)
WHOLE = pl.BlockSpec(memory_space=pltpu.VMEM)


def split_halves(x):
    high = x.astype(jnp.bfloat16)
    return high, (x - high.astype(jnp.float32)).astype(jnp.bfloat16)


def spread_kernel(ids_ref, out_ref):
    bag, per = ids_ref.shape
    half = bag // 2
    ids = jnp.concatenate([ids_ref[:half], ids_ref[half:]], axis=1)
    for j in range(half):
        out_ref[:, :, j * 2 * per : (j + 1) * 2 * per] = jnp.broadcast_to(
            ids[j : j + 1][None], (out_ref.shape[0], 1, 2 * per)
        )


def spread(ids, copies):
    bag, per = ids.shape
    return pl.pallas_call(
        spread_kernel,
        out_shape=jax.ShapeDtypeStruct((copies, 1, bag * per), jnp.int32),
        in_specs=[WHOLE],
        out_specs=WHOLE,
        compiler_params=PARAMS,
        name="spread",
    )(ids)


def count_kernel(bag, per, mate, places_ref, ids_ref, out_ref):
    half = bag // 2
    assert bag == 2 * half and half < 16
    rows = out_ref.shape[0] // 4
    pieces = 4 * rows // LANES
    words = pieces // 8
    part = 32
    low = 0x0F0F0F0F
    line_of = jnp.where(places_ref[8] == mate, 0, ids_ref.shape[0] // 2)

    def two_blocks(i, _):
        one, two = (
            jnp.concatenate([ids_ref[line_of + 2 * i + k, :, j * 2 * per : (j + 1) * 2 * per] for j in range(bag // 2)], axis=0)
            for k in range(2)
        )
        ids = jnp.concatenate(
            [
                jnp.concatenate([one[:, :per], two[:, :per]], axis=1),
                jnp.concatenate([one[:, per:], two[:, per:]], axis=1),
            ],
            axis=0,
        )
        columns = pl.ds(pl.multiple_of(i * LANES, LANES), LANES)
        line = ids & (LANES - 1)
        piece = jnp.full(ids.shape, -1, jnp.int32)
        for q in range(4):
            local = ids - places_ref[q]
            piece = jnp.where((local >= 0) & (local < rows), (q * rows + local) >> 7, piece)
        values = []
        for t in range(words):
            inside = (piece >= 8 * t) & (piece < 8 * (t + 1))
            values.append(jnp.where(inside, jnp.int32(1) << (piece & 7) * 4, 0))
        for first in range(0, LANES, part):
            lines = lax.broadcasted_iota(jnp.int32, (part, LANES), 0) + first
            sums = [[jnp.zeros((part, LANES), jnp.int32) for _ in range(words)] for _ in range(2)]
            for j in range(bag):
                hit = line[j : j + 1] == lines
                some = sums[j // half]
                for t in range(words):
                    some[t] = some[t] + jnp.where(hit, values[t][j : j + 1], 0)
            for t in range(words):
                one, two = sums[0][t], sums[1][t]
                even = (one & low) + (two & low)
                odd = ((one >> 4) & low) + ((two >> 4) & low)
                for f in range(8):
                    count = (even, odd)[f % 2] >> (f // 2 * 8)
                    if f < 6:
                        count = count & 255
                    at = (8 * t + f) * LANES + first
                    out_ref[at : at + part, columns] = count.astype(jnp.float32).astype(jnp.bfloat16)
        return 0

    lax.fori_loop(0, ids_ref.shape[0] // 4, two_blocks, 0)


def count_rows(places, ids, bag, per, rows, mate):
    return pl.pallas_call(
        functools.partial(count_kernel, bag, per, mate),
        out_shape=jax.ShapeDtypeStruct((4 * rows, ids.shape[0] // 2 * per), jnp.bfloat16),
        in_specs=[SCALARS, WHOLE],
        out_specs=WHOLE,
        compiler_params=PARAMS,
        name="count_rows",
    )(places, ids)


def pool_kernel(places_ref, counts_ref, own_ref, own_c_ref, far_ref, far_c_ref, out_ref, halves):
    rows, width = own_ref.shape
    for place, ref in ((4, own_ref), (5, own_c_ref), (6, far_ref), (7, far_c_ref)):
        high, low = split_halves(ref[...])
        lines = pl.ds(pl.multiple_of(places_ref[place] * rows, rows), rows)
        halves[lines, :width] = high
        halves[lines, width:] = low
    both = lax.dot_general(
        counts_ref[...], halves[...], (((0,), (0,)), ((), ())), preferred_element_type=jnp.float32
    )
    out_ref[...] = both[:, :width] + both[:, width:]


def pool(places, counts, tables):
    rows, width = tables[0].shape
    return pl.pallas_call(
        pool_kernel,
        out_shape=jax.ShapeDtypeStruct((counts.shape[1], width), jnp.float32),
        in_specs=[SCALARS] + [WHOLE] * 5,
        out_specs=WHOLE,
        scratch_shapes=[pltpu.VMEM((4 * rows, 2 * width), jnp.bfloat16)],
        compiler_params=PARAMS,
        name="pool",
    )(places, counts, *tables)


def dot3(a, b, dims):
    a_high, a_low = split_halves(a)
    b_high, b_low = split_halves(b)

    def dot(u, v):
        return lax.dot_general(u, v, (dims, ((), ())), preferred_element_type=jnp.float32)

    return dot(a_high, b_high) + (dot(a_high, b_low) + dot(a_low, b_high))


def cross_kernel(places_ref, parts_ref, weight_ref, bias_ref, upstream_ref, crossed_ref, keep_ref, give_ref):
    pooled = parts_ref[0]
    for k in range(1, parts_ref.shape[0]):
        pooled = pooled + parts_ref[k]
    weight, upstream = weight_ref[...], upstream_ref[...]
    mixed = dot3(pooled, weight, ((1,), (0,))) + bias_ref[...]
    crossed_ref[...] = pooled * mixed + pooled
    back = upstream * mixed + dot3(upstream * pooled, weight, ((1,), (1,))) + upstream
    half = keep_ref.shape[1]
    first = places_ref[8] == 0
    keep_ref[...] = jnp.where(first, back[:, :half], back[:, half:])
    give_ref[...] = jnp.where(first, back[:, half:], back[:, :half])


def cross(places, parts, weight, bias, upstream):
    samples, width = upstream.shape
    half = jax.ShapeDtypeStruct((samples, width // 2), jnp.float32)
    return pl.pallas_call(
        cross_kernel,
        out_shape=(jax.ShapeDtypeStruct(upstream.shape, jnp.float32), half, half),
        in_specs=[SCALARS] + [WHOLE] * 4,
        out_specs=(WHOLE, WHOLE, WHOLE),
        compiler_params=PARAMS,
        name="cross",
    )(places, parts, weight, bias.reshape(1, -1), upstream)


def row_kernel(core, near_ref, far_ref, back_ref, out_ref, halves):
    blocks, per, width = back_ref.shape
    per = per // 2
    for b in range(blocks):
        high, low = split_halves(back_ref[b])
        for k in range(2):
            halves[k, b * per : (b + 1) * per, :width] = high[k * per : (k + 1) * per]
            halves[k, b * per : (b + 1) * per, width:] = low[k * per : (k + 1) * per]
    rows = out_ref.shape[1]
    for h in range(2):
        chunk = slice((2 * h + core) * rows, (2 * h + core + 1) * rows)
        both = jnp.dot(near_ref[chunk, :], halves[0], preferred_element_type=jnp.float32)
        both = both + jnp.dot(far_ref[chunk, :], halves[1], preferred_element_type=jnp.float32)
        out_ref[h] = both[:, :width] + both[:, width:]


def row_sums(core, near, far, back, rows):
    width = back.shape[2]
    return pl.pallas_call(
        functools.partial(row_kernel, core),
        out_shape=jax.ShapeDtypeStruct((2, rows, width), jnp.float32),
        in_specs=[WHOLE] * 3,
        out_specs=WHOLE,
        scratch_shapes=[pltpu.VMEM((2, near.shape[1], 2 * width), jnp.bfloat16)],
        compiler_params=PARAMS,
        name="row_sums",
    )(near, far, back)


def merge_kernel(parts_ref, out_ref):
    total = parts_ref[0]
    for k in range(1, parts_ref.shape[0]):
        total = total + parts_ref[k]
    for k in range(out_ref.shape[0]):
        out_ref[k] = total


def merge(parts, copies):
    return pl.pallas_call(
        merge_kernel,
        out_shape=jax.ShapeDtypeStruct((copies,) + parts.shape[1:], jnp.float32),
        in_specs=[WHOLE],
        out_specs=WHOLE,
        compiler_params=PARAMS,
        name="merge",
    )(parts)


def adagrad_kernel(rows_ref, sums_ref, grads_ref, new_rows_ref, new_sums_ref):
    lines, width = rows_ref.shape
    half = width // 2
    at = (lines, lines)
    diagonal = lax.broadcasted_iota(jnp.int32, at, 0) == lax.broadcasted_iota(jnp.int32, at, 1)
    sums = jnp.sum(jnp.where(diagonal, sums_ref[0], 0.0), axis=1, keepdims=True)
    one, two = grads_ref[0], grads_ref[1]
    fresh = sums + jnp.sum(one * one + two * two, axis=1, keepdims=True) / width
    root = jnp.sqrt(fresh)
    new_rows_ref[:, :half] = rows_ref[:, :half] - 0.5 * one / root
    new_rows_ref[:, half:] = rows_ref[:, half:] - 0.5 * two / root
    new_sums_ref[0] = jnp.sum(jnp.where(diagonal, fresh, 0.0), axis=0, keepdims=True)


def adagrad(rows, sums, grads):
    count, width = rows.shape
    lines = 2 * LANES
    block = pl.BlockSpec((lines, width), lambda i: (i, 0))
    line = pl.BlockSpec((1, 1, lines), lambda i: (i, 0, 0))
    new_rows, new_sums = pl.pallas_call(
        adagrad_kernel,
        out_shape=(
            jax.ShapeDtypeStruct(rows.shape, jnp.float32),
            jax.ShapeDtypeStruct((count // lines, 1, lines), jnp.float32),
        ),
        grid=(count // lines,),
        in_specs=[block, line, pl.BlockSpec((2, lines, width // 2), lambda i: (0, i, 0))],
        out_specs=(block, line),
        compiler_params=PARAMS,
        name="adagrad",
    )(rows, sums.reshape(-1, 1, lines), grads)
    return new_rows, new_sums.reshape(-1)


def other_core(x):
    return lax.ppermute(x, "c", [(0, 1), (1, 0)])


def xl_mate(x):
    return lax.ppermute(x, "xl", [(0, 1), (1, 0)])


def x_neighbour(x):
    return lax.ppermute(x, ("xl", "xh"), [(0, 3), (3, 0), (1, 2), (2, 1)])


def body(bag_ids, table, accum, cross_weight, cross_bias, upstream):
    per, bag = bag_ids.shape
    rows, width = table.shape
    xl, xh, z, c = (lax.axis_index(a) for a in ("xl", "xh", "z", "c"))
    places = [(h * (NZ * 2) + z * 2 + d) * rows for h in (0, 1) for d in (c, 1 - c)]
    places = jnp.stack(places + [2 * xh, 2 * xh + 1, 2 - 2 * xh, 3 - 2 * xh, xl]).astype(jnp.int32)

    ids = lax.all_to_all(spread(bag_ids.T, 2 * NZ), ("xl", "z"), 0, 0, tiled=True)
    far = x_neighbour(table)
    own_c = other_core(table)
    far, ids, places = lax.optimization_barrier((far, ids, places))
    tables = (table, own_c, far, other_core(far))
    counts = count_rows(places, ids, bag, per, rows, 0)
    partial = pool(places, counts, tables)
    parts = lax.all_to_all(partial.reshape(NZ, per, width), "z", 0, 0, tiled=True)
    crossed, keep, give = cross(places, parts, cross_weight, cross_bias, upstream)
    ids, give = lax.optimization_barrier((ids, give))
    mate_counts = count_rows(places, ids, bag, per, rows, 1)

    halves = jnp.concatenate([keep, xl_mate(give)], axis=0)
    gathered = lax.all_gather(halves, "z", axis=0, tiled=False)
    theirs = other_core(row_sums(1, counts, mate_counts, gathered, rows))
    mine = row_sums(0, counts, mate_counts, gathered, rows) + theirs
    parts = lax.all_to_all(mine.reshape(16, rows // 8, width // 2), ("xh", "y"), 0, 0, tiled=True)
    totals = lax.all_to_all(merge(parts, 16), ("xl", "y"), 0, 0, tiled=True)
    new_table, new_accum = adagrad(table, accum, totals.reshape(2, rows, width // 2))
    return (crossed, new_table, new_accum)


def solution(mesh):
    fine = Mesh(mesh.devices.reshape(SIZES), AXES)
    samples = P(AXES, None)
    shard = ("xh", "z", "c")
    return jax.shard_map(
        body,
        mesh=fine,
        in_specs=(samples, P(shard, None), P(shard), P(), P(), samples),
        out_specs=(samples, P(shard, None), P(shard)),
        check_vma=False,
    )
```

```python
import functools

import jax
import jax.numpy as jnp
from jax import lax
from jax.experimental import pallas as pl
from jax.experimental.pallas import tpu as pltpu
from jax.sharding import Mesh
from jax.sharding import PartitionSpec as P

AXES = ("xl", "y", "xh", "z", "c")
SIZES = (2, 8, 2, 12, 2)
NZ = 12
LANES = 128
PARAMS = pltpu.CompilerParams(vmem_limit_bytes=16 * 1024 * 1024)
SCALARS = pl.BlockSpec(memory_space=pltpu.SMEM)
WHOLE = pl.BlockSpec(memory_space=pltpu.VMEM)


def split_halves(x):
    high = x.astype(jnp.bfloat16)
    return high, (x - high.astype(jnp.float32)).astype(jnp.bfloat16)


def spread_kernel(ids_ref, out_ref):
    bag, per = ids_ref.shape
    half = bag // 2
    ids = jnp.concatenate([ids_ref[:half], ids_ref[half:]], axis=1)
    for j in range(half):
        out_ref[:, :, j * 2 * per : (j + 1) * 2 * per] = jnp.broadcast_to(
            ids[j : j + 1][None], (out_ref.shape[0], 1, 2 * per)
        )


def spread(ids, copies):
    bag, per = ids.shape
    return pl.pallas_call(
        spread_kernel,
        out_shape=jax.ShapeDtypeStruct((copies, 1, bag * per), jnp.int32),
        in_specs=[WHOLE],
        out_specs=WHOLE,
        compiler_params=PARAMS,
        name="spread",
    )(ids)


def count_kernel(bag, per, mate, places_ref, ids_ref, out_ref):
    half = bag // 2
    assert bag == 2 * half and half < 16
    rows = out_ref.shape[0] // 4
    pieces = 4 * rows // LANES
    words = pieces // 8
    part = 32
    low = 0x0F0F0F0F
    line_of = jnp.where(places_ref[8] == mate, 0, ids_ref.shape[0] // 2)

    def two_blocks(i, _):
        one, two = (
            jnp.concatenate([ids_ref[line_of + 2 * i + k, :, j * 2 * per : (j + 1) * 2 * per] for j in range(bag // 2)], axis=0)
            for k in range(2)
        )
        ids = jnp.concatenate(
            [
                jnp.concatenate([one[:, :per], two[:, :per]], axis=1),
                jnp.concatenate([one[:, per:], two[:, per:]], axis=1),
            ],
            axis=0,
        )
        columns = pl.ds(pl.multiple_of(i * LANES, LANES), LANES)
        line = ids & (LANES - 1)
        piece = jnp.full(ids.shape, -1, jnp.int32)
        for q in range(4):
            local = ids - places_ref[q]
            piece = jnp.where((local >= 0) & (local < rows), (q * rows + local) >> 7, piece)
        values = []
        for t in range(words):
            inside = (piece >= 8 * t) & (piece < 8 * (t + 1))
            values.append(jnp.where(inside, jnp.int32(1) << (piece & 7) * 4, 0))
        for first in range(0, LANES, part):
            lines = lax.broadcasted_iota(jnp.int32, (part, LANES), 0) + first
            sums = [[jnp.zeros((part, LANES), jnp.int32) for _ in range(words)] for _ in range(2)]
            for j in range(bag):
                hit = line[j : j + 1] == lines
                some = sums[j // half]
                for t in range(words):
                    some[t] = some[t] + jnp.where(hit, values[t][j : j + 1], 0)
            for t in range(words):
                one, two = sums[0][t], sums[1][t]
                even = (one & low) + (two & low)
                odd = ((one >> 4) & low) + ((two >> 4) & low)
                for f in range(8):
                    count = (even, odd)[f % 2] >> (f // 2 * 8)
                    if f < 6:
                        count = count & 255
                    at = (8 * t + f) * LANES + first
                    out_ref[at : at + part, columns] = count.astype(jnp.float32).astype(jnp.bfloat16)
        return 0

    lax.fori_loop(0, ids_ref.shape[0] // 4, two_blocks, 0)


def count_rows(places, ids, bag, per, rows, mate):
    return pl.pallas_call(
        functools.partial(count_kernel, bag, per, mate),
        out_shape=jax.ShapeDtypeStruct((4 * rows, ids.shape[0] // 2 * per), jnp.bfloat16),
        in_specs=[SCALARS, WHOLE],
        out_specs=WHOLE,
        compiler_params=PARAMS,
        cost_estimate=pl.CostEstimate(flops=2000000000, bytes_accessed=0, transcendentals=0),
        name="count_rows",
    )(places, ids)


def pool_kernel(places_ref, counts_ref, own_ref, own_c_ref, far_ref, far_c_ref, out_ref, halves):
    rows, width = own_ref.shape
    for place, ref in ((4, own_ref), (5, own_c_ref), (6, far_ref), (7, far_c_ref)):
        high, low = split_halves(ref[...])
        lines = pl.ds(pl.multiple_of(places_ref[place] * rows, rows), rows)
        halves[lines, :width] = high
        halves[lines, width:] = low
    both = lax.dot_general(
        counts_ref[...], halves[...], (((0,), (0,)), ((), ())), preferred_element_type=jnp.float32
    )
    out_ref[...] = both[:, :width] + both[:, width:]


def pool(places, counts, tables):
    rows, width = tables[0].shape
    return pl.pallas_call(
        pool_kernel,
        out_shape=jax.ShapeDtypeStruct((counts.shape[1], width), jnp.float32),
        in_specs=[SCALARS] + [WHOLE] * 5,
        out_specs=WHOLE,
        scratch_shapes=[pltpu.VMEM((4 * rows, 2 * width), jnp.bfloat16)],
        compiler_params=PARAMS,
        name="pool",
    )(places, counts, *tables)


def dot3(a, b, dims):
    a_high, a_low = split_halves(a)
    b_high, b_low = split_halves(b)

    def dot(u, v):
        return lax.dot_general(u, v, (dims, ((), ())), preferred_element_type=jnp.float32)

    return dot(a_high, b_high) + (dot(a_high, b_low) + dot(a_low, b_high))


def cross_kernel(places_ref, parts_ref, weight_ref, bias_ref, upstream_ref, crossed_ref, keep_ref, give_ref):
    pooled = parts_ref[0]
    for k in range(1, parts_ref.shape[0]):
        pooled = pooled + parts_ref[k]
    weight, upstream = weight_ref[...], upstream_ref[...]
    mixed = dot3(pooled, weight, ((1,), (0,))) + bias_ref[...]
    crossed_ref[...] = pooled * mixed + pooled
    back = upstream * mixed + dot3(upstream * pooled, weight, ((1,), (1,))) + upstream
    half = keep_ref.shape[1]
    first = places_ref[8] == 0
    keep_ref[...] = jnp.where(first, back[:, :half], back[:, half:])
    give_ref[...] = jnp.where(first, back[:, half:], back[:, :half])


def cross(places, parts, weight, bias, upstream):
    samples, width = upstream.shape
    half = jax.ShapeDtypeStruct((samples, width // 2), jnp.float32)
    return pl.pallas_call(
        cross_kernel,
        out_shape=(jax.ShapeDtypeStruct(upstream.shape, jnp.float32), half, half),
        in_specs=[SCALARS] + [WHOLE] * 4,
        out_specs=(WHOLE, WHOLE, WHOLE),
        compiler_params=PARAMS,
        name="cross",
    )(places, parts, weight, bias.reshape(1, -1), upstream)


def row_kernel(core, near_ref, far_ref, back_ref, out_ref, halves):
    blocks, per, width = back_ref.shape
    per = per // 2
    for b in range(blocks):
        high, low = split_halves(back_ref[b])
        for k in range(2):
            halves[k, b * per : (b + 1) * per, :width] = high[k * per : (k + 1) * per]
            halves[k, b * per : (b + 1) * per, width:] = low[k * per : (k + 1) * per]
    rows = out_ref.shape[1]
    for h in range(2):
        chunk = slice((2 * h + core) * rows, (2 * h + core + 1) * rows)
        both = jnp.dot(near_ref[chunk, :], halves[0], preferred_element_type=jnp.float32)
        both = both + jnp.dot(far_ref[chunk, :], halves[1], preferred_element_type=jnp.float32)
        out_ref[h] = both[:, :width] + both[:, width:]


def row_sums(core, near, far, back, rows):
    width = back.shape[2]
    return pl.pallas_call(
        functools.partial(row_kernel, core),
        out_shape=jax.ShapeDtypeStruct((2, rows, width), jnp.float32),
        in_specs=[WHOLE] * 3,
        out_specs=WHOLE,
        scratch_shapes=[pltpu.VMEM((2, near.shape[1], 2 * width), jnp.bfloat16)],
        compiler_params=PARAMS,
        name="row_sums",
    )(near, far, back)


def merge_kernel(parts_ref, out_ref):
    total = parts_ref[0]
    for k in range(1, parts_ref.shape[0]):
        total = total + parts_ref[k]
    for k in range(out_ref.shape[0]):
        out_ref[k] = total


def merge(parts, copies):
    return pl.pallas_call(
        merge_kernel,
        out_shape=jax.ShapeDtypeStruct((copies,) + parts.shape[1:], jnp.float32),
        in_specs=[WHOLE],
        out_specs=WHOLE,
        compiler_params=PARAMS,
        name="merge",
    )(parts)


def adagrad_kernel(rows_ref, sums_ref, grads_ref, new_rows_ref, new_sums_ref):
    lines, width = rows_ref.shape
    half = width // 2
    at = (lines, lines)
    diagonal = lax.broadcasted_iota(jnp.int32, at, 0) == lax.broadcasted_iota(jnp.int32, at, 1)
    sums = jnp.sum(jnp.where(diagonal, sums_ref[0], 0.0), axis=1, keepdims=True)
    one, two = grads_ref[0], grads_ref[1]
    fresh = sums + jnp.sum(one * one + two * two, axis=1, keepdims=True) / width
    root = jnp.sqrt(fresh)
    new_rows_ref[:, :half] = rows_ref[:, :half] - 0.5 * one / root
    new_rows_ref[:, half:] = rows_ref[:, half:] - 0.5 * two / root
    new_sums_ref[0] = jnp.sum(jnp.where(diagonal, fresh, 0.0), axis=0, keepdims=True)


def adagrad(rows, sums, grads):
    count, width = rows.shape
    lines = 2 * LANES
    block = pl.BlockSpec((lines, width), lambda i: (i, 0))
    line = pl.BlockSpec((1, 1, lines), lambda i: (i, 0, 0))
    new_rows, new_sums = pl.pallas_call(
        adagrad_kernel,
        out_shape=(
            jax.ShapeDtypeStruct(rows.shape, jnp.float32),
            jax.ShapeDtypeStruct((count // lines, 1, lines), jnp.float32),
        ),
        grid=(count // lines,),
        in_specs=[block, line, pl.BlockSpec((2, lines, width // 2), lambda i: (0, i, 0))],
        out_specs=(block, line),
        compiler_params=PARAMS,
        name="adagrad",
    )(rows, sums.reshape(-1, 1, lines), grads)
    return new_rows, new_sums.reshape(-1)


def other_core(x):
    return lax.ppermute(x, "c", [(0, 1), (1, 0)])


def xl_mate(x):
    return lax.ppermute(x, "xl", [(0, 1), (1, 0)])


def x_neighbour(x):
    return lax.ppermute(x, ("xl", "xh"), [(0, 3), (3, 0), (1, 2), (2, 1)])


def body(bag_ids, table, accum, cross_weight, cross_bias, upstream):
    per, bag = bag_ids.shape
    rows, width = table.shape
    xl, xh, z, c = (lax.axis_index(a) for a in ("xl", "xh", "z", "c"))
    places = [(h * (NZ * 2) + z * 2 + d) * rows for h in (0, 1) for d in (c, 1 - c)]
    places = jnp.stack(places + [2 * xh, 2 * xh + 1, 2 - 2 * xh, 3 - 2 * xh, xl]).astype(jnp.int32)

    ids = lax.all_to_all(spread(bag_ids.T, 2 * NZ), ("xl", "z"), 0, 0, tiled=True)
    far = x_neighbour(table)
    own_c = other_core(table)
    ids, places = lax.optimization_barrier((ids, places))
    tables = (table, own_c, far, other_core(far))
    counts = count_rows(places, ids, bag, per, rows, 0)
    partial = pool(places, counts, tables)
    parts = lax.all_to_all(partial.reshape(NZ, per, width), "z", 0, 0, tiled=True)
    crossed, keep, give = cross(places, parts, cross_weight, cross_bias, upstream)
    ids, give = lax.optimization_barrier((ids, give))
    mate_counts = count_rows(places, ids, bag, per, rows, 1)

    halves = jnp.concatenate([keep, xl_mate(give)], axis=0)
    gathered = lax.all_gather(halves, "z", axis=0, tiled=False)
    theirs = other_core(row_sums(1, counts, mate_counts, gathered, rows))
    mine = row_sums(0, counts, mate_counts, gathered, rows) + theirs
    parts = lax.all_to_all(mine.reshape(16, rows // 8, width // 2), ("xh", "y"), 0, 0, tiled=True)
    totals = lax.all_to_all(merge(parts, 16), ("xl", "y"), 0, 0, tiled=True)
    new_table, new_accum = adagrad(table, accum, totals.reshape(2, rows, width // 2))
    return (crossed, new_table, new_accum)


def solution(mesh):
    fine = Mesh(mesh.devices.reshape(SIZES), AXES)
    samples = P(AXES, None)
    shard = ("xh", "z", "c")
    return jax.shard_map(
        body,
        mesh=fine,
        in_specs=(samples, P(shard, None), P(shard), P(), P(), samples),
        out_specs=(samples, P(shard, None), P(shard)),
        check_vma=False,
    )
```

```python
import functools

import jax
import jax.numpy as jnp
from jax import lax
from jax.experimental import pallas as pl
from jax.experimental.pallas import tpu as pltpu
from jax.sharding import Mesh
from jax.sharding import PartitionSpec as P

AXES = ("xl", "y", "xh", "z", "c")
SIZES = (2, 8, 2, 12, 2)
NZ = 12
LANES = 128
PARAMS = pltpu.CompilerParams(vmem_limit_bytes=16 * 1024 * 1024)
SCALARS = pl.BlockSpec(memory_space=pltpu.SMEM)
WHOLE = pl.BlockSpec(memory_space=pltpu.VMEM)


def split_halves(x):
    high = x.astype(jnp.bfloat16)
    return high, (x - high.astype(jnp.float32)).astype(jnp.bfloat16)


def spread_kernel(ids_ref, out_ref):
    bag, per = ids_ref.shape
    half = bag // 2
    ids = jnp.concatenate([ids_ref[:half], ids_ref[half:]], axis=1)
    for j in range(half):
        out_ref[:, :, j * 2 * per : (j + 1) * 2 * per] = jnp.broadcast_to(
            ids[j : j + 1][None], (out_ref.shape[0], 1, 2 * per)
        )


def spread(ids, copies):
    bag, per = ids.shape
    return pl.pallas_call(
        spread_kernel,
        out_shape=jax.ShapeDtypeStruct((copies, 1, bag * per), jnp.int32),
        in_specs=[WHOLE],
        out_specs=WHOLE,
        compiler_params=PARAMS,
        name="spread",
    )(ids)


def count_kernel(bag, per, mate, places_ref, ids_ref, out_ref):
    half = bag // 2
    assert bag == 2 * half and half < 16
    rows = out_ref.shape[0] // 4
    pieces = 4 * rows // LANES
    words = pieces // 8
    part = 32
    low = 0x0F0F0F0F
    line_of = jnp.where(places_ref[8] == mate, 0, ids_ref.shape[0] // 2)

    def two_blocks(i, _):
        one, two = (
            jnp.concatenate([ids_ref[line_of + 2 * i + k, :, j * 2 * per : (j + 1) * 2 * per] for j in range(bag // 2)], axis=0)
            for k in range(2)
        )
        ids = jnp.concatenate(
            [
                jnp.concatenate([one[:, :per], two[:, :per]], axis=1),
                jnp.concatenate([one[:, per:], two[:, per:]], axis=1),
            ],
            axis=0,
        )
        columns = pl.ds(pl.multiple_of(i * LANES, LANES), LANES)
        line = ids & (LANES - 1)
        piece = jnp.full(ids.shape, -1, jnp.int32)
        for q in range(4):
            local = ids - places_ref[q]
            piece = jnp.where((local >= 0) & (local < rows), (q * rows + local) >> 7, piece)
        values = []
        for t in range(words):
            inside = (piece >= 8 * t) & (piece < 8 * (t + 1))
            values.append(jnp.where(inside, jnp.int32(1) << (piece & 7) * 4, 0))
        for first in range(0, LANES, part):
            lines = lax.broadcasted_iota(jnp.int32, (part, LANES), 0) + first
            sums = [[jnp.zeros((part, LANES), jnp.int32) for _ in range(words)] for _ in range(2)]
            for j in range(bag):
                hit = line[j : j + 1] == lines
                some = sums[j // half]
                for t in range(words):
                    some[t] = some[t] + jnp.where(hit, values[t][j : j + 1], 0)
            for t in range(words):
                one, two = sums[0][t], sums[1][t]
                even = (one & low) + (two & low)
                odd = ((one >> 4) & low) + ((two >> 4) & low)
                for f in range(8):
                    count = (even, odd)[f % 2] >> (f // 2 * 8)
                    if f < 6:
                        count = count & 255
                    at = (8 * t + f) * LANES + first
                    out_ref[at : at + part, columns] = count.astype(jnp.float32).astype(jnp.bfloat16)
        return 0

    lax.fori_loop(0, ids_ref.shape[0] // 4, two_blocks, 0)


def count_rows(places, ids, bag, per, rows, mate):
    return pl.pallas_call(
        functools.partial(count_kernel, bag, per, mate),
        out_shape=jax.ShapeDtypeStruct((4 * rows, ids.shape[0] // 2 * per), jnp.bfloat16),
        in_specs=[SCALARS, WHOLE],
        out_specs=WHOLE,
        compiler_params=PARAMS,
        cost_estimate=pl.CostEstimate(flops=2000000000, bytes_accessed=0, transcendentals=0),
        name="count_rows",
    )(places, ids)


def pool_kernel(places_ref, counts_ref, own_ref, own_c_ref, far_ref, far_c_ref, out_ref, halves):
    rows, width = own_ref.shape
    for place, ref in ((4, own_ref), (5, own_c_ref), (6, far_ref), (7, far_c_ref)):
        high, low = split_halves(ref[...])
        lines = pl.ds(pl.multiple_of(places_ref[place] * rows, rows), rows)
        halves[lines, :width] = high
        halves[lines, width:] = low
    both = lax.dot_general(
        counts_ref[...], halves[...], (((0,), (0,)), ((), ())), preferred_element_type=jnp.float32
    )
    out_ref[...] = both[:, :width] + both[:, width:]


def pool(places, counts, tables):
    rows, width = tables[0].shape
    return pl.pallas_call(
        pool_kernel,
        out_shape=jax.ShapeDtypeStruct((counts.shape[1], width), jnp.float32),
        in_specs=[SCALARS] + [WHOLE] * 5,
        out_specs=WHOLE,
        scratch_shapes=[pltpu.VMEM((4 * rows, 2 * width), jnp.bfloat16)],
        compiler_params=PARAMS,
        name="pool",
    )(places, counts, *tables)


def dot3(a, b, dims):
    rows = a.shape[0]
    a_both = jnp.concatenate(split_halves(a), axis=0)
    b_high, b_low = split_halves(b)

    def dot(u, v):
        return lax.dot_general(u, v, (dims, ((), ())), preferred_element_type=jnp.float32)

    by_high = dot(a_both, b_high)
    return by_high[:rows] + (dot(a_both[:rows], b_low) + by_high[rows:])


def cross_kernel(places_ref, parts_ref, weight_ref, bias_ref, upstream_ref, crossed_ref, keep_ref, give_ref):
    pooled = parts_ref[0]
    for k in range(1, parts_ref.shape[0]):
        pooled = pooled + parts_ref[k]
    weight, upstream = weight_ref[...], upstream_ref[...]
    mixed = dot3(pooled, weight, ((1,), (0,))) + bias_ref[...]
    crossed_ref[...] = pooled * mixed + pooled
    back = upstream * mixed + dot3(upstream * pooled, weight, ((1,), (1,))) + upstream
    half = keep_ref.shape[1]
    first = places_ref[8] == 0
    keep_ref[...] = jnp.where(first, back[:, :half], back[:, half:])
    give_ref[...] = jnp.where(first, back[:, half:], back[:, :half])


def cross(places, parts, weight, bias, upstream):
    samples, width = upstream.shape
    half = jax.ShapeDtypeStruct((samples, width // 2), jnp.float32)
    return pl.pallas_call(
        cross_kernel,
        out_shape=(jax.ShapeDtypeStruct(upstream.shape, jnp.float32), half, half),
        in_specs=[SCALARS] + [WHOLE] * 4,
        out_specs=(WHOLE, WHOLE, WHOLE),
        compiler_params=PARAMS,
        name="cross",
    )(places, parts, weight, bias.reshape(1, -1), upstream)


def row_sums_of(core, near_ref, mate_ref, halves, out_ref):
    _, rows, width = out_ref.shape
    for h in range(2):
        chunk = slice((2 * h + core) * rows, (2 * h + core + 1) * rows)
        both = jnp.dot(near_ref[chunk, :], halves[0], preferred_element_type=jnp.float32)
        both = both + jnp.dot(mate_ref[chunk, :], halves[1], preferred_element_type=jnp.float32)
        out_ref[h] = both[:, :width] + both[:, width:]


def their_rows_kernel(near_ref, mate_ref, back_ref, out_ref, halves):
    blocks, per, width = back_ref.shape
    per = per // 2
    for b in range(blocks):
        high, low = split_halves(back_ref[b])
        for k in range(2):
            halves[k, b * per : (b + 1) * per, :width] = high[k * per : (k + 1) * per]
            halves[k, b * per : (b + 1) * per, width:] = low[k * per : (k + 1) * per]
    row_sums_of(1, near_ref, mate_ref, halves, out_ref)


def their_rows(near, mate, back, rows):
    width = back.shape[2]
    return pl.pallas_call(
        their_rows_kernel,
        out_shape=(
            jax.ShapeDtypeStruct((2, rows, width), jnp.float32),
            jax.ShapeDtypeStruct((2, near.shape[1], 2 * width), jnp.bfloat16),
        ),
        in_specs=[WHOLE] * 3,
        out_specs=(WHOLE, WHOLE),
        compiler_params=PARAMS,
        name="their_rows",
    )(near, mate, back)


def own_rows(near, mate, halves, rows):
    return pl.pallas_call(
        functools.partial(row_sums_of, 0),
        out_shape=jax.ShapeDtypeStruct((2, rows, halves.shape[2] // 2), jnp.float32),
        in_specs=[WHOLE] * 3,
        out_specs=WHOLE,
        compiler_params=PARAMS,
        name="own_rows",
    )(near, mate, halves)


def merge_kernel(parts_ref, out_ref):
    total = parts_ref[0]
    for k in range(1, parts_ref.shape[0]):
        total = total + parts_ref[k]
    for k in range(out_ref.shape[0]):
        out_ref[k] = total


def merge(parts, copies):
    return pl.pallas_call(
        merge_kernel,
        out_shape=jax.ShapeDtypeStruct((copies,) + parts.shape[1:], jnp.float32),
        in_specs=[WHOLE],
        out_specs=WHOLE,
        compiler_params=PARAMS,
        name="merge",
    )(parts)


def adagrad_kernel(rows_ref, sums_ref, grads_ref, new_rows_ref, new_sums_ref):
    lines, width = rows_ref.shape
    half = width // 2
    at = (lines, lines)
    diagonal = lax.broadcasted_iota(jnp.int32, at, 0) == lax.broadcasted_iota(jnp.int32, at, 1)
    sums = jnp.sum(jnp.where(diagonal, sums_ref[0], 0.0), axis=1, keepdims=True)
    one, two = grads_ref[0], grads_ref[1]
    fresh = sums + jnp.sum(one * one + two * two, axis=1, keepdims=True) / width
    root = jnp.sqrt(fresh)
    new_rows_ref[:, :half] = rows_ref[:, :half] - 0.5 * one / root
    new_rows_ref[:, half:] = rows_ref[:, half:] - 0.5 * two / root
    new_sums_ref[0] = jnp.sum(jnp.where(diagonal, fresh, 0.0), axis=0, keepdims=True)


def adagrad(rows, sums, grads):
    count, width = rows.shape
    lines = 2 * LANES
    block = pl.BlockSpec((lines, width), lambda i: (i, 0))
    line = pl.BlockSpec((1, 1, lines), lambda i: (i, 0, 0))
    new_rows, new_sums = pl.pallas_call(
        adagrad_kernel,
        out_shape=(
            jax.ShapeDtypeStruct(rows.shape, jnp.float32),
            jax.ShapeDtypeStruct((count // lines, 1, lines), jnp.float32),
        ),
        grid=(count // lines,),
        in_specs=[block, line, pl.BlockSpec((2, lines, width // 2), lambda i: (0, i, 0))],
        out_specs=(block, line),
        compiler_params=PARAMS,
        name="adagrad",
    )(rows, sums.reshape(-1, 1, lines), grads)
    return new_rows, new_sums.reshape(-1)


def other_core(x):
    return lax.ppermute(x, "c", [(0, 1), (1, 0)])


def xl_mate(x):
    return lax.ppermute(x, "xl", [(0, 1), (1, 0)])


def x_neighbour(x):
    return lax.ppermute(x, ("xl", "xh"), [(0, 3), (3, 0), (1, 2), (2, 1)])


def body(bag_ids, table, accum, cross_weight, cross_bias, upstream):
    per, bag = bag_ids.shape
    rows, width = table.shape
    xl, xh, z, c = (lax.axis_index(a) for a in ("xl", "xh", "z", "c"))
    places = [(h * (NZ * 2) + z * 2 + d) * rows for h in (0, 1) for d in (c, 1 - c)]
    places = jnp.stack(places + [2 * xh, 2 * xh + 1, 2 - 2 * xh, 3 - 2 * xh, xl]).astype(jnp.int32)

    ids = lax.all_to_all(spread(bag_ids.T, 2 * NZ), ("xl", "z"), 0, 0, tiled=True)
    far = x_neighbour(table)
    own_c = other_core(table)
    ids, places = lax.optimization_barrier((ids, places))
    tables = (table, own_c, far, other_core(far))
    counts = count_rows(places, ids, bag, per, rows, 0)
    partial = pool(places, counts, tables)
    parts = lax.all_to_all(partial.reshape(NZ, per, width), "z", 0, 0, tiled=True)
    crossed, keep, give = cross(places, parts, cross_weight, cross_bias, upstream)
    ids, give = lax.optimization_barrier((ids, give))
    mate_counts = count_rows(places, ids, bag, per, rows, 1)

    both = jnp.concatenate([keep, xl_mate(give)], axis=0)
    gathered = lax.all_gather(both, "z", axis=0, tiled=False)
    theirs, halves = their_rows(counts, mate_counts, gathered, rows)
    theirs = other_core(theirs)
    mine = own_rows(counts, mate_counts, halves, rows) + theirs
    parts = lax.all_to_all(mine.reshape(16, rows // 8, width // 2), ("xh", "y"), 0, 0, tiled=True)
    totals = lax.all_to_all(merge(parts, 16), ("xl", "y"), 0, 0, tiled=True)
    new_table, new_accum = adagrad(table, accum, totals.reshape(2, rows, width // 2))
    return (crossed, new_table, new_accum)


def solution(mesh):
    fine = Mesh(mesh.devices.reshape(SIZES), AXES)
    samples = P(AXES, None)
    shard = ("xh", "z", "c")
    return jax.shard_map(
        body,
        mesh=fine,
        in_specs=(samples, P(shard, None), P(shard), P(), P(), samples),
        out_specs=(samples, P(shard, None), P(shard)),
        check_vma=False,
    )
```

```python
import functools

import jax
import jax.numpy as jnp
from jax import lax
from jax.experimental import pallas as pl
from jax.experimental.pallas import tpu as pltpu
from jax.sharding import Mesh
from jax.sharding import PartitionSpec as P

AXES = ("xl", "y", "xh", "z", "c")
SIZES = (2, 8, 2, 12, 2)
NZ = 12
LANES = 128
PARAMS = pltpu.CompilerParams(vmem_limit_bytes=16 * 1024 * 1024)
SCALARS = pl.BlockSpec(memory_space=pltpu.SMEM)
WHOLE = pl.BlockSpec(memory_space=pltpu.VMEM)


def split_halves(x):
    high = x.astype(jnp.bfloat16)
    return high, (x - high.astype(jnp.float32)).astype(jnp.bfloat16)


def spread_kernel(ids_ref, out_ref):
    bag, per = ids_ref.shape
    half = bag // 2
    ids = jnp.concatenate([ids_ref[:half], ids_ref[half:]], axis=1)
    for j in range(half):
        out_ref[:, :, j * 2 * per : (j + 1) * 2 * per] = jnp.broadcast_to(
            ids[j : j + 1][None], (out_ref.shape[0], 1, 2 * per)
        )


def spread(ids, copies):
    bag, per = ids.shape
    return pl.pallas_call(
        spread_kernel,
        out_shape=jax.ShapeDtypeStruct((copies, 1, bag * per), jnp.int32),
        in_specs=[WHOLE],
        out_specs=WHOLE,
        compiler_params=PARAMS,
        name="spread",
    )(ids)


def count_kernel(bag, per, mate, places_ref, ids_ref, out_ref):
    half = bag // 2
    assert bag == 2 * half and half < 16
    rows = out_ref.shape[0] // 4
    pieces = 4 * rows // LANES
    words = pieces // 8
    part = 32
    low = 0x0F0F0F0F
    line_of = jnp.where(places_ref[8] == mate, 0, ids_ref.shape[0] // 2)

    def two_blocks(i, _):
        one, two = (
            jnp.concatenate([ids_ref[line_of + 2 * i + k, :, j * 2 * per : (j + 1) * 2 * per] for j in range(bag // 2)], axis=0)
            for k in range(2)
        )
        ids = jnp.concatenate(
            [
                jnp.concatenate([one[:, :per], two[:, :per]], axis=1),
                jnp.concatenate([one[:, per:], two[:, per:]], axis=1),
            ],
            axis=0,
        )
        columns = pl.ds(pl.multiple_of(i * LANES, LANES), LANES)
        line = ids & (LANES - 1)
        piece = jnp.full(ids.shape, -1, jnp.int32)
        for q in range(4):
            local = ids - places_ref[q]
            piece = jnp.where((local >= 0) & (local < rows), (q * rows + local) >> 7, piece)
        values = []
        for t in range(words):
            inside = (piece >= 8 * t) & (piece < 8 * (t + 1))
            values.append(jnp.where(inside, jnp.int32(1) << (piece & 7) * 4, 0))
        for first in range(0, LANES, part):
            lines = lax.broadcasted_iota(jnp.int32, (part, LANES), 0) + first
            sums = [[jnp.zeros((part, LANES), jnp.int32) for _ in range(words)] for _ in range(2)]
            for j in range(bag):
                hit = line[j : j + 1] == lines
                some = sums[j // half]
                for t in range(words):
                    some[t] = some[t] + jnp.where(hit, values[t][j : j + 1], 0)
            for t in range(words):
                one, two = sums[0][t], sums[1][t]
                even = (one & low) + (two & low)
                odd = ((one >> 4) & low) + ((two >> 4) & low)
                for f in range(8):
                    count = (even, odd)[f % 2] >> (f // 2 * 8)
                    if f < 6:
                        count = count & 255
                    at = (8 * t + f) * LANES + first
                    out_ref[at : at + part, columns] = count.astype(jnp.float32).astype(jnp.bfloat16)
        return 0

    lax.fori_loop(0, ids_ref.shape[0] // 4, two_blocks, 0)


def count_rows(places, ids, bag, per, rows, mate):
    return pl.pallas_call(
        functools.partial(count_kernel, bag, per, mate),
        out_shape=jax.ShapeDtypeStruct((4 * rows, ids.shape[0] // 2 * per), jnp.bfloat16),
        in_specs=[SCALARS, WHOLE],
        out_specs=WHOLE,
        compiler_params=PARAMS,
        cost_estimate=pl.CostEstimate(flops=2000000000, bytes_accessed=0, transcendentals=0),
        name="count_rows",
    )(places, ids)


def pool_kernel(places_ref, counts_ref, own_ref, own_c_ref, far_ref, far_c_ref, out_ref, halves):
    rows, width = own_ref.shape
    for place, ref in ((4, own_ref), (5, own_c_ref), (6, far_ref), (7, far_c_ref)):
        high, low = split_halves(ref[...])
        lines = pl.ds(pl.multiple_of(places_ref[place] * rows, rows), rows)
        halves[lines, :width] = high
        halves[lines, width:] = low
    both = lax.dot_general(
        counts_ref[...], halves[...], (((0,), (0,)), ((), ())), preferred_element_type=jnp.float32
    )
    out_ref[...] = both[:, :width] + both[:, width:]


def pool(places, counts, tables):
    rows, width = tables[0].shape
    return pl.pallas_call(
        pool_kernel,
        out_shape=jax.ShapeDtypeStruct((counts.shape[1], width), jnp.float32),
        in_specs=[SCALARS] + [WHOLE] * 5,
        out_specs=WHOLE,
        scratch_shapes=[pltpu.VMEM((4 * rows, 2 * width), jnp.bfloat16)],
        compiler_params=PARAMS,
        name="pool",
    )(places, counts, *tables)


def dot3(a, b, dims):
    rows = a.shape[0]
    a_both = jnp.concatenate(split_halves(a), axis=0)
    b_high, b_low = split_halves(b)

    def dot(u, v):
        return lax.dot_general(u, v, (dims, ((), ())), preferred_element_type=jnp.float32)

    by_high = dot(a_both, b_high)
    return by_high[:rows] + (dot(a_both[:rows], b_low) + by_high[rows:])


def cross_kernel(places_ref, parts_ref, weight_ref, bias_ref, upstream_ref, crossed_ref, keep_ref, give_ref):
    pooled = parts_ref[0]
    for k in range(1, parts_ref.shape[0]):
        pooled = pooled + parts_ref[k]
    weight, upstream = weight_ref[...], upstream_ref[...]
    mixed = dot3(pooled, weight, ((1,), (0,))) + bias_ref[...]
    crossed_ref[...] = pooled * mixed + pooled
    back = upstream * mixed + dot3(upstream * pooled, weight, ((1,), (1,))) + upstream
    half = keep_ref.shape[1]
    first = places_ref[8] == 0
    keep_ref[...] = jnp.where(first, back[:, :half], back[:, half:])
    give_ref[...] = jnp.where(first, back[:, half:], back[:, :half])


def cross(places, parts, weight, bias, upstream):
    samples, width = upstream.shape
    half = jax.ShapeDtypeStruct((samples, width // 2), jnp.float32)
    return pl.pallas_call(
        cross_kernel,
        out_shape=(jax.ShapeDtypeStruct(upstream.shape, jnp.float32), half, half),
        in_specs=[SCALARS] + [WHOLE] * 4,
        out_specs=(WHOLE, WHOLE, WHOLE),
        compiler_params=PARAMS,
        name="cross",
    )(places, parts, weight, bias.reshape(1, -1), upstream)


def row_sums_of(core, near_ref, mate_ref, halves, out_ref):
    _, rows, width = out_ref.shape
    for h in range(2):
        chunk = slice((2 * h + core) * rows, (2 * h + core + 1) * rows)
        both = jnp.dot(near_ref[chunk, :], halves[0], preferred_element_type=jnp.float32)
        both = both + jnp.dot(mate_ref[chunk, :], halves[1], preferred_element_type=jnp.float32)
        out_ref[h] = both[:, :width] + both[:, width:]


def their_rows_kernel(near_ref, mate_ref, back_ref, out_ref, halves):
    blocks, per, width = back_ref.shape
    per = per // 2
    for b in range(blocks):
        high, low = split_halves(back_ref[b])
        for k in range(2):
            halves[k, b * per : (b + 1) * per, :width] = high[k * per : (k + 1) * per]
            halves[k, b * per : (b + 1) * per, width:] = low[k * per : (k + 1) * per]
    row_sums_of(1, near_ref, mate_ref, halves, out_ref)


def their_rows(near, mate, back, rows):
    width = back.shape[2]
    return pl.pallas_call(
        their_rows_kernel,
        out_shape=(
            jax.ShapeDtypeStruct((2, rows, width), jnp.float32),
            jax.ShapeDtypeStruct((2, near.shape[1], 2 * width), jnp.bfloat16),
        ),
        in_specs=[WHOLE] * 3,
        out_specs=(WHOLE, WHOLE),
        compiler_params=PARAMS,
        name="their_rows",
    )(near, mate, back)


def own_rows(near, mate, halves, rows):
    return pl.pallas_call(
        functools.partial(row_sums_of, 0),
        out_shape=jax.ShapeDtypeStruct((2, rows, halves.shape[2] // 2), jnp.float32),
        in_specs=[WHOLE] * 3,
        out_specs=WHOLE,
        compiler_params=PARAMS,
        name="own_rows",
    )(near, mate, halves)


def merge_kernel(parts_ref, out_ref):
    total = parts_ref[0]
    for k in range(1, parts_ref.shape[0]):
        total = total + parts_ref[k]
    for k in range(out_ref.shape[0]):
        out_ref[k] = total


def merge(parts, copies):
    return pl.pallas_call(
        merge_kernel,
        out_shape=jax.ShapeDtypeStruct((copies,) + parts.shape[1:], jnp.float32),
        in_specs=[WHOLE],
        out_specs=WHOLE,
        compiler_params=PARAMS,
        name="merge",
    )(parts)


def adagrad_kernel(rows_ref, sums_ref, grads_ref, new_rows_ref, new_sums_ref):
    width = rows_ref.shape[1]
    half = width // 2
    at = (LANES, LANES)
    diagonal = lax.broadcasted_iota(jnp.int32, at, 0) == lax.broadcasted_iota(jnp.int32, at, 1)
    for k in range(sums_ref.shape[0]):
        lines = slice(k * LANES, (k + 1) * LANES)
        sums = jnp.sum(jnp.where(diagonal, sums_ref[k], 0.0), axis=1, keepdims=True)
        one, two = grads_ref[0, lines, :], grads_ref[1, lines, :]
        fresh = sums + jnp.sum(one * one + two * two, axis=1, keepdims=True) / width
        scale = 0.5 / jnp.sqrt(fresh)
        new_rows_ref[lines, :half] = rows_ref[lines, :half] - one * scale
        new_rows_ref[lines, half:] = rows_ref[lines, half:] - two * scale
        new_sums_ref[k] = jnp.sum(jnp.where(diagonal, fresh, 0.0), axis=0, keepdims=True)


def adagrad(rows, sums, grads):
    sums = sums.reshape(-1, 1, LANES)
    new_rows, new_sums = pl.pallas_call(
        adagrad_kernel,
        out_shape=(
            jax.ShapeDtypeStruct(rows.shape, jnp.float32),
            jax.ShapeDtypeStruct(sums.shape, jnp.float32),
        ),
        in_specs=[WHOLE] * 3,
        out_specs=(WHOLE, WHOLE),
        compiler_params=PARAMS,
        name="adagrad",
    )(rows, sums, grads)
    return new_rows, new_sums.reshape(-1)


def other_core(x):
    return lax.ppermute(x, "c", [(0, 1), (1, 0)])


def xl_mate(x):
    return lax.ppermute(x, "xl", [(0, 1), (1, 0)])


def x_neighbour(x):
    return lax.ppermute(x, ("xl", "xh"), [(0, 3), (3, 0), (1, 2), (2, 1)])


def body(bag_ids, table, accum, cross_weight, cross_bias, upstream):
    per, bag = bag_ids.shape
    rows, width = table.shape
    xl, xh, z, c = (lax.axis_index(a) for a in ("xl", "xh", "z", "c"))
    places = [(h * (NZ * 2) + z * 2 + d) * rows for h in (0, 1) for d in (c, 1 - c)]
    places = jnp.stack(places + [2 * xh, 2 * xh + 1, 2 - 2 * xh, 3 - 2 * xh, xl]).astype(jnp.int32)

    ids = lax.all_to_all(spread(bag_ids.T, 2 * NZ), ("xl", "z"), 0, 0, tiled=True)
    far = x_neighbour(table)
    own_c = other_core(table)
    ids, places = lax.optimization_barrier((ids, places))
    tables = (table, own_c, far, other_core(far))
    counts = count_rows(places, ids, bag, per, rows, 0)
    partial = pool(places, counts, tables)
    parts = lax.all_to_all(partial.reshape(NZ, per, width), "z", 0, 0, tiled=True)
    crossed, keep, give = cross(places, parts, cross_weight, cross_bias, upstream)
    ids, give = lax.optimization_barrier((ids, give))
    mate_counts = count_rows(places, ids, bag, per, rows, 1)

    both = jnp.concatenate([keep, xl_mate(give)], axis=0)
    gathered = lax.all_gather(both, "z", axis=0, tiled=False)
    theirs, halves = their_rows(counts, mate_counts, gathered, rows)
    theirs = other_core(theirs)
    mine = own_rows(counts, mate_counts, halves, rows) + theirs
    parts = lax.all_to_all(mine.reshape(16, rows // 8, width // 2), ("xh", "y"), 0, 0, tiled=True)
    totals = lax.all_to_all(merge(parts, 16), ("xl", "y"), 0, 0, tiled=True)
    new_table, new_accum = adagrad(table, accum, totals.reshape(2, rows, width // 2))
    return (crossed, new_table, new_accum)


def solution(mesh):
    fine = Mesh(mesh.devices.reshape(SIZES), AXES)
    samples = P(AXES, None)
    shard = ("xh", "z", "c")
    return jax.shard_map(
        body,
        mesh=fine,
        in_specs=(samples, P(shard, None), P(shard), P(), P(), samples),
        out_specs=(samples, P(shard, None), P(shard)),
        check_vma=False,
    )
```
